128 devices in a mesh: seq: 8 (over x, core), node: 16 (over y, z).
Axes of the slice: x: 4, y: 4, z: 4, core: 2. Of those that a mesh axis runs over, the one named last changes fastest.
Arguments:
- queries: float32 [131072, 1024], P(('seq', 'node')), may hold values from -9 to 9
- keys: float32 [131072, 1024], P(('seq', 'node')), may hold values from -9 to 9
- values: float32 [131072, 1024], P(('seq', 'node')), may hold values from -6 to 6
Outputs:
- attended: float32 [131072, 1024], P(('seq', 'node'))
The draws below stay inside these ranges and needn't reach their ends.
All inputs are finite; a program needn't handle non-finite values.
Results may differ from the reference program's by a relative error of at most 0.0003.
Values sent between devices are 32-bit elements; how exact they have to be, the bound alone decides.
No kernel may reach another device: no remote copies, remote signals or barrier semaphores. Data moves between devices by JAX's collectives and lax.ppermute only.
A program may use at most 192 MiB of HBM per device.

```python
import math
import jax
import jax.numpy as jnp
from jax import lax

HEADS = 8
CHANNEL_WIDTH = 128
D = 1024
SEGMENT_LENGTH = 128
TOKENS = 131072


def draw_queries(key, part):
    key = jax.random.fold_in(key, 5)
    result = jax.random.normal(key, (TOKENS, D), dtype=jnp.float32)
    return jnp.clip(result, -9.0, 9.0).astype(jnp.float32)


def draw_keys(key, part):
    key = jax.random.fold_in(key, 7)
    result = jax.random.normal(key, (TOKENS, D), dtype=jnp.float32)
    return jnp.clip(result, -9.0, 9.0).astype(jnp.float32)


def block_levels(key, extent, cuts, least, high):
    def one(dim, shards_of):
        draws = jax.random.uniform(jax.random.fold_in(jax.random.fold_in(key, 6), dim), (shards_of,), jnp.float32, least / len(cuts), high / len(cuts))
        return jnp.repeat(jnp.exp(draws), extent[dim] // shards_of).reshape((-1,) + (1,) * (len(extent) - dim - 1))

    gain = one(*cuts[0])
    for cut in cuts[1:]:
        gain = gain * one(*cut)
    return gain


def gaussian(key, extent, spread, most, cuts=(), kind=jnp.bfloat16):
    array = jax.random.normal(key, extent, jnp.float32) * spread
    if len(cuts) > 0:
        array = block_levels(key, extent, cuts, -0.22, 0.18) * array
    return jnp.clip(array, min=-most, max=most).astype(kind)


def setup_inputs(seed: int = 0) -> dict:
    splits = jax.random.split(jax.random.key(seed), 4)
    return {
        "queries": draw_queries(jax.random.fold_in(splits[3], 71), 0),
        "keys": draw_keys(jax.random.fold_in(splits[3], 71), 0),
        "values": gaussian(splits[2], (TOKENS, D), 1.0, 6.0, ((0, 128),), jnp.float32),
    }


NATURAL_LN_DUO = math.log(2.0)


def pool_pairs(matrix):
    paired = matrix.reshape(matrix.shape[0] // 2, 2, matrix.shape[1])
    return 0.5 * (paired[:, 0] + paired[:, 1])


def mix_sibling_segments(probe_entries, lookup_entries, payload_entries, logit_offset):
    row_count = probe_entries.shape[0]
    col_count = lookup_entries.shape[0]
    query_heads = probe_entries.reshape(row_count, HEADS, CHANNEL_WIDTH)
    key_heads = lookup_entries.reshape(col_count, HEADS, CHANNEL_WIDTH)
    value_heads = payload_entries.reshape(col_count, HEADS, CHANNEL_WIDTH)
    logit_grid = jnp.einsum("rhd,chd->hrc", query_heads, key_heads, precision=lax.Precision.HIGHEST)
    logit_grid = logit_grid * (CHANNEL_WIDTH ** -0.5) + logit_offset
    peak = jnp.max(logit_grid, axis=2)
    weights = jnp.exp(logit_grid - peak[:, :, None])
    weight_sum = jnp.sum(weights, axis=2)
    numerator = jnp.einsum("hrc,chd->rhd", weights, value_heads, precision=lax.Precision.HIGHEST)
    return peak.T, weight_sum.T, numerator


def level_parts(level_q, level_k, level_v, hierarchy_depth):
    pair_count = level_q.shape[0] // (2 * SEGMENT_LENGTH)
    shape = (pair_count, 2 * SEGMENT_LENGTH, level_q.shape[1])
    logit_offset = hierarchy_depth * NATURAL_LN_DUO

    def one_pair(items):
        coupled_probes, coupled_lookups, coupled_payloads = items
        if hierarchy_depth == 0:
            return mix_sibling_segments(coupled_probes, coupled_lookups, coupled_payloads, 0.0)
        leading_portion = mix_sibling_segments(coupled_probes[:SEGMENT_LENGTH], coupled_lookups[SEGMENT_LENGTH:], coupled_payloads[SEGMENT_LENGTH:], logit_offset)
        trailing_portion = mix_sibling_segments(coupled_probes[SEGMENT_LENGTH:], coupled_lookups[:SEGMENT_LENGTH], coupled_payloads[:SEGMENT_LENGTH], logit_offset)
        return tuple(jnp.concatenate([one_item, two_item], axis=0) for one_item, two_item in zip(leading_portion, trailing_portion))

    peak, weight_sum, numerator = lax.map(one_pair, (level_q.reshape(shape), level_k.reshape(shape), level_v.reshape(shape)))
    row_count = level_q.shape[0]
    factor = 2 ** hierarchy_depth
    peak = jnp.repeat(peak.reshape(row_count, HEADS), factor, axis=0)
    weight_sum = jnp.repeat(weight_sum.reshape(row_count, HEADS), factor, axis=0)
    numerator = jnp.repeat(numerator.reshape(row_count, HEADS, CHANNEL_WIDTH), factor, axis=0)
    return peak, weight_sum, numerator


def combine_parts(running, addition):
    peak_a, sum_a, num_a = running
    peak_b, sum_b, num_b = addition
    peak = jnp.maximum(peak_a, peak_b)
    scale_a = jnp.exp(peak_a - peak)
    scale_b = jnp.exp(peak_b - peak)
    return peak, sum_a * scale_a + sum_b * scale_b, num_a * scale_a[:, :, None] + num_b * scale_b[:, :, None]


def reference(queries, keys, values):
    level_count = (TOKENS // SEGMENT_LENGTH).bit_length() - 1
    level_q, level_k, level_v = queries, keys, values
    running = level_parts(level_q, level_k, level_v, 0)
    for hierarchy_depth in range(1, level_count):
        level_q = pool_pairs(level_q)
        level_k = pool_pairs(level_k)
        level_v = pool_pairs(level_v)
        running = combine_parts(running, level_parts(level_q, level_k, level_v, hierarchy_depth))
    peak, weight_sum, numerator = running
    return (numerator / weight_sum[:, :, None]).reshape(TOKENS, HEADS * CHANNEL_WIDTH)
```

```python
import functools
import math

import jax
import jax.numpy as jnp
from jax import lax
from jax.experimental import pallas as pl
from jax.experimental.pallas import tpu as pltpu
from jax.sharding import PartitionSpec as P

HEADS = 8
WIDTH = 128
ROWS = 1024
F32 = jnp.float32
BF16 = jnp.bfloat16
SCALE = WIDTH ** (-0.5) / math.log(2.0)
VMEM_LIMIT = 48 * 1024 * 1024

GROUPS = [list(range(8)), [12, 13, 14, 15, 8, 9, 10, 11]]


def params():
    return pltpu.CompilerParams(vmem_limit_bytes=VMEM_LIMIT)


def split(x):
    hi = x.astype(BF16)
    lo = (x - hi.astype(F32)).astype(BF16)
    return hi, lo


def dot_nt(a, b):
    return lax.dot_general(a, b, (((1,), (1,)), ((), ())), preferred_element_type=F32)


def dot_nn(a, b):
    return lax.dot_general(a, b, (((1,), (0,)), ((), ())), preferred_element_type=F32)


def key_side(k):
    hi, lo = split(k)
    return jnp.concatenate([hi, hi], axis=1), jnp.concatenate([lo, jnp.zeros_like(lo)], axis=1)


def scores(q, sides):
    hi, lo = split(q)
    both = jnp.concatenate([hi, lo], axis=1)
    first, second = sides
    n = first.shape[0]
    if n == 128:
        s = dot_nt(both, jnp.concatenate([first, second], axis=0))
        return s[:, :n] + s[:, n:]
    return dot_nt(both, first) + dot_nt(both, second)


def value_side(v):
    hi, lo = split(v)
    return hi, lo


def weigh(p, side):
    hi, lo = side
    p_hi, p_lo = split(p)
    if hi.shape[0] == 128:
        left = jnp.concatenate([p_hi, p_lo], axis=1)
        right = jnp.concatenate(
            [jnp.concatenate([hi, lo], axis=1), jnp.concatenate([hi, jnp.zeros_like(lo)], axis=1)], axis=0
        )
        r = dot_nn(left, right)
        return r[:, :WIDTH] + r[:, WIDTH:]
    r = dot_nn(p_hi, jnp.concatenate([hi, lo], axis=1))
    return r[:, :WIDTH] + r[:, WIDTH:] + dot_nn(p_lo, hi)


def attend(q, k_side, v_side, level):
    s = scores(q, k_side)
    peak = jnp.max(s, axis=1, keepdims=True)
    p = jnp.exp2(s - peak)
    total = jnp.sum(p, axis=1, keepdims=True)
    return peak + float(level), total, weigh(p, v_side)


def merge(a, b):
    ma, sa, na = a
    mb, sb, nb = b
    gap = ma - mb
    small = jnp.exp2(-jnp.abs(gap))
    fa = jnp.where(gap >= 0, 1.0, small)
    fb = jnp.where(gap >= 0, small, 1.0)
    return jnp.maximum(ma, mb), sa * fa + sb * fb, na * fa + nb * fb


def pool_body(q_ref, k_ref, v_ref, q3_ref, kv3_ref, kv4_ref, pay_ref, scratch):
    def level3(ref):
        total = ref[pl.ds(0, 128, stride=8), :]
        for k in range(1, 8):
            total = total + ref[pl.ds(k, 128, stride=8), :]
        return total * 0.125

    def halve(ref, n):
        return 0.5 * (ref[pl.ds(0, n, stride=2), :] + ref[pl.ds(1, n, stride=2), :])

    q3 = level3(q_ref) * SCALE
    k3 = level3(k_ref)
    v3 = level3(v_ref)
    q3_ref[...] = q3
    kv3_ref[0] = k3
    kv3_ref[1] = v3
    for i, x in enumerate((q3, k3, v3)):
        scratch[i, 0:128, :] = x
        x4 = halve(scratch.at[i, 0:128], 64)
        scratch[i, 128:192, :] = x4
        if i > 0:
            kv4_ref[i - 1] = x4
        pay_ref[0, 32 * i : 32 * i + 32, :] = halve(scratch.at[i, 128:192], 32)


def pool_call(q, k, v):
    block = pl.BlockSpec((ROWS, WIDTH), lambda h: (0, h))
    return pl.pallas_call(
        pool_body,
        name="pool_rows",
        grid=(HEADS,),
        in_specs=[block] * 3,
        out_specs=[
            pl.BlockSpec((128, WIDTH), lambda h: (0, h)),
            pl.BlockSpec((2, 128, WIDTH), lambda h: (0, 0, h)),
            pl.BlockSpec((2, 64, WIDTH), lambda h: (0, 0, h)),
            pl.BlockSpec((1, 96, WIDTH), lambda h: (h, 0, 0)),
        ],
        out_shape=[
            jax.ShapeDtypeStruct((128, HEADS * WIDTH), F32),
            jax.ShapeDtypeStruct((2, 128, HEADS * WIDTH), F32),
            jax.ShapeDtypeStruct((2, 64, HEADS * WIDTH), F32),
            jax.ShapeDtypeStruct((HEADS, 96, WIDTH), F32),
        ],
        scratch_shapes=[pltpu.VMEM((3, 192, WIDTH), F32)],
        compiler_params=params(),
        cost_estimate=pl.CostEstimate(flops=3 << 20, bytes_accessed=14 << 20, transcendentals=0),
    )(q, k, v)


def local_body(q_ref, k_ref, v_ref, o_ref, lse_ref):
    head = pl.program_id(0)

    def load(ref):
        return [ref[pl.ds(k, 128, stride=8), :] for k in range(8)]

    def pool(parts):
        return [0.5 * (parts[2 * i] + parts[2 * i + 1]) for i in range(len(parts) // 2)]

    def rows(parts, first, count):
        return jnp.concatenate([x[first : first + count] for x in parts], axis=0)

    q0 = [x * SCALE for x in load(q_ref)]
    k0, v0 = load(k_ref), load(v_ref)
    q1, k1, v1 = pool(q0), pool(k0), pool(v0)
    q2, k2, v2 = pool(q1), pool(k1), pool(v1)

    at2 = []
    for b in range(2):
        c = b ^ 1
        at2.append(attend(rows(q2, 64 * b, 64), key_side(rows(k2, 64 * c, 64)), value_side(rows(v2, 64 * c, 64)), 2))

    lane = lax.broadcasted_iota(jnp.int32, (128, WIDTH), 1)
    lses = [[None] * 4 for _ in range(8)]
    for p in range(4):
        c = p ^ 1
        m1, s1, n1 = attend(
            rows(q1, 32 * p, 32), key_side(rows(k1, 32 * c, 32)), value_side(rows(v1, 32 * c, 32)), 1
        )
        m0, s0, n0 = attend(
            rows(q0, 32 * p, 32), key_side(rows(k0, 32 * p, 32)), value_side(rows(v0, 32 * p, 32)), 0
        )
        off = 32 * (p % 2)
        for j in range(4):
            i = j // 2
            one = tuple(x[32 * j : 32 * j + 32] for x in (m1, s1, n1))
            two = tuple(x[64 * i + off : 64 * i + off + 32] for x in at2[p // 2])
            coarse = merge(one, two)
            for k in (2 * j, 2 * j + 1):
                zero = tuple(x[32 * k : 32 * k + 32] for x in (m0, s0, n0))
                m, s, n = merge(zero, coarse)
                o_ref[128 * k + 32 * p : 128 * k + 32 * p + 32, :] = n / s
                lses[k][p] = m + jnp.log2(s)
    for k in range(8):
        old = lse_ref[128 * k : 128 * k + 128, :]
        lse_ref[128 * k : 128 * k + 128, :] = jnp.where(lane == head, jnp.concatenate(lses[k], axis=0), old)


def local_call(q, k, v):
    block = pl.BlockSpec((ROWS, WIDTH), lambda h: (0, h))
    return pl.pallas_call(
        local_body,
        name="local_levels",
        grid=(HEADS,),
        in_specs=[block] * 3,
        out_specs=[block, pl.BlockSpec((ROWS, WIDTH), lambda h: (0, 0))],
        out_shape=[
            jax.ShapeDtypeStruct((ROWS, HEADS * WIDTH), F32),
            jax.ShapeDtypeStruct((ROWS, WIDTH), F32),
        ],
        compiler_params=params(),
        cost_estimate=pl.CostEstimate(flops=4 << 30, bytes_accessed=16 << 20, transcendentals=3 << 20),
    )(q, k, v)


def near_body(q3_ref, kv3_ref, kv4a_ref, kv4b_ref, o_ref, lse_ref, scratch, *, step):
    group = pl.program_id(0)
    lane = lax.broadcasted_iota(jnp.int32, (128, WIDTH), 1)
    packed = lse_ref[...]
    for h in range(step):
        cols = slice(WIDTH * h, WIDTH * h + WIDTH)
        scratch[h, 0, :, :] = q3_ref[:, cols]
        q4 = 0.5 * (scratch[h, 0, pl.ds(0, 64, stride=2), :] + scratch[h, 0, pl.ds(1, 64, stride=2), :])
        k4 = jnp.concatenate([kv4a_ref[0, :, cols], kv4b_ref[0, :, cols]], axis=0)
        v4 = jnp.concatenate([kv4a_ref[1, :, cols], kv4b_ref[1, :, cols]], axis=0)
        m4, s4, n4 = attend(q4, key_side(k4), value_side(v4), 4)
        for i, x in enumerate((m4, s4, n4)):
            x = jnp.broadcast_to(x, (64, WIDTH))
            scratch[h, i + 1, pl.ds(0, 64, stride=2), :] = x
            scratch[h, i + 1, pl.ds(1, 64, stride=2), :] = x
        three = attend(q3_ref[:, cols], key_side(kv3_ref[0, :, cols]), value_side(kv3_ref[1, :, cols]), 3)
        m, s, n = merge(three, (scratch[h, 1], scratch[h, 2], scratch[h, 3]))
        o_ref[:, cols] = n / s
        packed = jnp.where(lane == group * step + h, m + jnp.log2(s), packed)
    lse_ref[...] = packed


def near_call(q3, kv3, kv4a, kv4b):
    step = 4
    wide = step * WIDTH
    return pl.pallas_call(
        functools.partial(near_body, step=step),
        name="near_levels",
        grid=(HEADS // step,),
        in_specs=[
            pl.BlockSpec((128, wide), lambda h: (0, h)),
            pl.BlockSpec((2, 128, wide), lambda h: (0, 0, h)),
            pl.BlockSpec((2, 64, wide), lambda h: (0, 0, h)),
            pl.BlockSpec((2, 64, wide), lambda h: (0, 0, h)),
        ],
        out_specs=[pl.BlockSpec((128, wide), lambda h: (0, h)), pl.BlockSpec((128, WIDTH), lambda h: (0, 0))],
        out_shape=[
            jax.ShapeDtypeStruct((128, HEADS * WIDTH), F32),
            jax.ShapeDtypeStruct((128, WIDTH), F32),
        ],
        scratch_shapes=[pltpu.VMEM((step, 4, 128, WIDTH), F32)],
        compiler_params=params(),
        cost_estimate=pl.CostEstimate(flops=400 << 20, bytes_accessed=4 << 20, transcendentals=1 << 18),
    )(q3, kv3, kv4a, kv4b)


def rise_body(got_ref, a6_ref, a7_ref, a8_ref, a9_ref, scratch):
    outs = (a6_ref, a7_ref, a8_ref, a9_ref)
    for i in range(2):
        for s in range(8):
            scratch[32 * s : 32 * s + 32, :] = got_ref[s, 32 * (i + 1) : 32 * (i + 2), :]
        count, base = 128, 0
        for ref in outs:
            x = 0.5 * (
                scratch[pl.ds(base, count, stride=2), :] + scratch[pl.ds(base + 1, count, stride=2), :]
            )
            ref[i] = x
            base = base + 2 * count
            if count > 16:
                scratch[base : base + count, :] = x
            count = count // 2


def rise_call(got):
    return pl.pallas_call(
        rise_body,
        name="rise_rows",
        out_shape=[jax.ShapeDtypeStruct((2, n, WIDTH), F32) for n in (128, 64, 32, 16)],
        scratch_shapes=[pltpu.VMEM((512, WIDTH), F32)],
        compiler_params=params(),
        cost_estimate=pl.CostEstimate(flops=1 << 18, bytes_accessed=1 << 19, transcendentals=0),
    )(got)


def far_body(got_ref, kv6_ref, near_ref, across_ref, out_ref, qs, es):
    q5 = jnp.concatenate([got_ref[s, 0:32, :] for s in range(8)], axis=0)
    qs[0:256, :] = q5
    base, count = 0, 128
    queries = [q5]
    while count >= 16:
        x = 0.5 * (qs[pl.ds(base, count, stride=2), :] + qs[pl.ds(base + 1, count, stride=2), :])
        queries.append(x)
        base = base + 2 * count
        if count > 16:
            qs[base : base + count, :] = x
        count = count // 2

    def keys(i, first, count):
        return jnp.concatenate([near_ref[i, first : first + count], across_ref[i, first : first + count]], axis=0)

    results = []
    for g in range(2):
        other = range(4) if g == 1 else range(4, 8)
        k5 = jnp.concatenate([got_ref[s, 32:64, :] for s in other], axis=0)
        v5 = jnp.concatenate([got_ref[s, 64:96, :] for s in other], axis=0)
        results.append(attend(q5[128 * g : 128 * g + 128], key_side(k5), value_side(v5), 5))
    five = tuple(jnp.concatenate([a, b], axis=0) for a, b in zip(*results))
    levels = [five, attend(queries[1], key_side(kv6_ref[0]), value_side(kv6_ref[1]), 6)]
    for i in range(3):
        levels.append(
            attend(queries[2 + i], key_side(keys(0, 64 * i, 64)), value_side(keys(1, 64 * i, 64)), 7 + i)
        )
    running = levels[-1]
    base = 0
    for finer in reversed(levels[:-1]):
        n = running[0].shape[0]
        wide = []
        for i, x in enumerate(running):
            x = jnp.broadcast_to(x, (n, WIDTH))
            es[i, pl.ds(base, n, stride=2), :] = x
            es[i, pl.ds(base + 1, n, stride=2), :] = x
            wide.append(es[i, base : base + 2 * n, :])
        base = base + 2 * n
        running = merge(finer, tuple(wide))
    m, s, n = running
    o = n / s
    lse = jnp.broadcast_to(m + jnp.log2(s), (256, WIDTH))
    for d in range(8):
        out_ref[d, 0:32, :] = o[32 * d : 32 * d + 32]
        out_ref[d, 32:64, :] = lse[32 * d : 32 * d + 32]


def far_call(got, kv6, near, across):
    return pl.pallas_call(
        far_body,
        name="far_levels",
        out_shape=jax.ShapeDtypeStruct((HEADS, 64, WIDTH), F32),
        scratch_shapes=[pltpu.VMEM((512, WIDTH), F32), pltpu.VMEM((3, 512, WIDTH), F32)],
        compiler_params=params(),
        cost_estimate=pl.CostEstimate(flops=100 << 20, bytes_accessed=1 << 20, transcendentals=1 << 17),
    )(got, kv6, near, across)


def join_body(o_ref, lse_ref, o34_ref, lse34_ref, far_ref, out_ref, scratch):
    head = pl.program_id(0)
    lane = lax.broadcasted_iota(jnp.int32, (128, WIDTH), 1)

    def pick(x):
        return jnp.sum(jnp.where(lane == head, x, 0.0), axis=1, keepdims=True)

    for i in range(2):
        x = far_ref[0, 32 * i : 32 * i + 32, :]
        for c in range(4):
            scratch[i, pl.ds(c, 32, stride=4), :] = x
    m, s, n = merge((pick(lse34_ref[...]), 1.0, o34_ref[...]), (scratch[1], 1.0, scratch[0]))
    for k in range(8):
        own = (pick(lse_ref[128 * k : 128 * k + 128, :]), 1.0, o_ref[128 * k : 128 * k + 128, :])
        _, den, num = merge(own, (m, s, n))
        out_ref[pl.ds(k, 128, stride=8), :] = num / den


def join_call(o, lse, o34, lse34, far):
    block = pl.BlockSpec((ROWS, WIDTH), lambda h: (0, h))
    return pl.pallas_call(
        join_body,
        name="join_levels",
        grid=(HEADS,),
        in_specs=[
            block,
            pl.BlockSpec((ROWS, WIDTH), lambda h: (0, 0)),
            pl.BlockSpec((128, WIDTH), lambda h: (0, h)),
            pl.BlockSpec((128, WIDTH), lambda h: (0, 0)),
            pl.BlockSpec((1, 64, WIDTH), lambda h: (h, 0, 0)),
        ],
        out_specs=block,
        out_shape=jax.ShapeDtypeStruct((ROWS, HEADS * WIDTH), F32),
        scratch_shapes=[pltpu.VMEM((2, 128, WIDTH), F32)],
        compiler_params=params(),
        cost_estimate=pl.CostEstimate(flops=16 << 20, bytes_accessed=9 << 20, transcendentals=1 << 20),
    )(o, lse, o34, lse34, far)


def hop(x, axis, flip):
    return lax.ppermute(x, axis, [(i, i ^ flip) for i in range(lax.axis_size(axis))])


def transpose_heads(x):
    return lax.all_to_all(x, "node", 0, 0, axis_index_groups=GROUPS, tiled=True)


def on_device(queries, keys, values):
    q3, kv3, kv4, pay = pool_call(queries, keys, values)
    got = transpose_heads(pay)
    got, kv3, kv4 = lax.optimization_barrier((got, kv3, kv4))
    o, lse = local_call(queries, keys, values)
    a6, a7, a8, a9 = rise_call(got)

    r8 = hop(a8, "seq", 2)
    r9a = hop(a9, "seq", 4)
    r9b = hop(a9, "seq", 6)
    kv6 = hop(a6, "node", 12)
    c7 = hop(a7, "seq", 1)
    fetched = jnp.concatenate([r8, r9a, r9b], axis=1)
    passed = hop(fetched, "seq", 1)
    near = jnp.concatenate([c7, fetched[:, :32], passed[:, :32], fetched[:, 32:], passed[:, 32:]], axis=1)
    across = hop(near, "node", 12)

    sib3 = hop(kv3, "node", 1)
    sib4a = hop(kv4, "node", 3)
    sib4b = hop(kv4, "node", 2)

    far = far_call(got, kv6, near, across)
    back = transpose_heads(far)
    o34, lse34 = near_call(q3, sib3, sib4a, sib4b)
    return join_call(o, lse, o34, lse34, back)


def solution(mesh):
    spec = P(("seq", "node"), None)
    return jax.shard_map(on_device, mesh=mesh, in_specs=(spec, spec, spec), out_specs=spec, check_vma=False)
```

```python
import functools
import math

import jax
import jax.numpy as jnp
from jax import lax
from jax.experimental import pallas as pl
from jax.experimental.pallas import tpu as pltpu
from jax.sharding import PartitionSpec as P

HEADS = 8
CALLS = (2, 1, 5)
WIDTH = 128
ROWS = 1024
F32 = jnp.float32
BF16 = jnp.bfloat16
SCALE = WIDTH ** (-0.5) / math.log(2.0)
MIB = 1024 * 1024

GROUPS = [list(range(8)), [12, 13, 14, 15, 8, 9, 10, 11]]


def params(mib=12):
    return pltpu.CompilerParams(vmem_limit_bytes=mib * MIB)


def in_hbm(x):
    return pltpu.with_memory_space_constraint(x, pltpu.HBM)


def split(x):
    hi = x.astype(BF16)
    lo = (x - hi.astype(F32)).astype(BF16)
    return hi, lo


def dot_nt(a, b):
    return lax.dot_general(a, b, (((1,), (1,)), ((), ())), preferred_element_type=F32)


def dot_nn(a, b):
    return lax.dot_general(a, b, (((1,), (0,)), ((), ())), preferred_element_type=F32)


def key_side(k):
    hi, lo = split(k)
    return jnp.concatenate([hi, hi], axis=1), jnp.concatenate([lo, jnp.zeros_like(lo)], axis=1)


def scores(q, sides):
    hi, lo = split(q)
    both = jnp.concatenate([hi, lo], axis=1)
    first, second = sides
    n = first.shape[0]
    if n == 128:
        s = dot_nt(both, jnp.concatenate([first, second], axis=0))
        return s[:, :n] + s[:, n:]
    return dot_nt(both, first) + dot_nt(both, second)


def weigh(p, side):
    hi, lo = side
    p_hi, p_lo = split(p)
    if hi.shape[0] == 128:
        left = jnp.concatenate([p_hi, p_lo], axis=1)
        right = jnp.concatenate(
            [jnp.concatenate([hi, lo], axis=1), jnp.concatenate([hi, jnp.zeros_like(lo)], axis=1)], axis=0
        )
        r = dot_nn(left, right)
        return r[:, :WIDTH] + r[:, WIDTH:]
    r = dot_nn(p_hi, jnp.concatenate([hi, lo], axis=1))
    return r[:, :WIDTH] + r[:, WIDTH:] + dot_nn(p_lo, hi)


def attend_all(tasks):
    grids = [scores(q, key_side(k)) for q, k, _, _ in tasks]
    peaks = [jnp.max(s, axis=1, keepdims=True) for s in grids]
    weights = [jnp.exp2(s - peak) for s, peak in zip(grids, peaks)]
    totals = [jnp.sum(p, axis=1, keepdims=True) for p in weights]
    numerators = [weigh(p, split(task[2])) for p, task in zip(weights, tasks)]
    return [(peak + float(task[3]), t, n) for peak, t, n, task in zip(peaks, totals, numerators, tasks)]


def merge(a, b):
    ma, sa, na = a
    mb, sb, nb = b
    gap = ma - mb
    small = jnp.exp2(-jnp.abs(gap))
    fa = jnp.where(gap >= 0, 1.0, small)
    fb = jnp.where(gap >= 0, small, 1.0)
    return jnp.maximum(ma, mb), sa * fa + sb * fb, na * fa + nb * fb


def pool_body(q_hbm, k_hbm, v_hbm, q3_ref, mean_ref, half_ref, pay_ref, rows, scratch, sems):
    arrays = (q_hbm, k_hbm, v_hbm)

    def fetch(i, h):
        return pltpu.make_async_copy(
            arrays[i].at[:, WIDTH * h : WIDTH * h + WIDTH], rows.at[i, h], sems.at[i, h]
        )

    for h in range(HEADS):
        for i in range(3):
            fetch(i, h).start()

    def pairs(ref, n):
        return 0.5 * ref[pl.ds(0, n, stride=2), :], 0.5 * ref[pl.ds(1, n, stride=2), :]

    for h in range(HEADS):
        cols = slice(WIDTH * h, WIDTH * h + WIDTH)
        for i in range(3):
            fetch(i, h).wait()
            ref = rows.at[i, h]
            total = ref[pl.ds(0, 128, stride=8), :]
            for k in range(1, 8):
                total = total + ref[pl.ds(k, 128, stride=8), :]
            x = total * (0.125 * SCALE if i == 0 else 0.125)
            scratch[i, 0:128, :] = x
            even, odd = pairs(scratch.at[i, 0:128], 64)
            scratch[i, 128:192, :] = even + odd
            pay_ref[h, 32 * i : 32 * i + 32, :] = sum(pairs(scratch.at[i, 128:192], 32))
            if i == 0:
                q3_ref[:, cols] = x
            else:
                mean_ref[i - 1, :, cols] = even + odd
                half_ref[i - 1, :, cols] = even - odd


def pool_call(q, k, v):
    return pl.pallas_call(
        pool_body,
        name="pool_rows",
        in_specs=[pl.BlockSpec(memory_space=pl.ANY)] * 3,
        out_shape=[
            pltpu.HBM((128, HEADS * WIDTH), F32),
            pltpu.HBM((2, 64, HEADS * WIDTH), F32),
            pltpu.HBM((2, 64, HEADS * WIDTH), F32),
            pltpu.HBM((HEADS, 96, WIDTH), F32),
        ],
        scratch_shapes=[
            pltpu.VMEM((3, HEADS, ROWS, WIDTH), F32),
            pltpu.VMEM((3, 192, WIDTH), F32),
            pltpu.SemaphoreType.DMA((3, HEADS)),
        ],
        compiler_params=params(24),
        cost_estimate=pl.CostEstimate(flops=3 << 20, bytes_accessed=14 << 20, transcendentals=0),
    )(in_hbm(q), in_hbm(k), in_hbm(v))


def local_body(first, q_ref, k_ref, v_ref, o_ref, lse_ref):
    head = pl.program_id(0) + first

    def load(ref):
        return [ref[pl.ds(k, 128, stride=8), :] for k in range(8)]

    def pool(parts):
        return [0.5 * (parts[2 * i] + parts[2 * i + 1]) for i in range(len(parts) // 2)]

    def rows(parts, begin, count):
        return jnp.concatenate([x[begin : begin + count] for x in parts], axis=0)

    q0 = [x * SCALE for x in load(q_ref)]
    k0, v0 = load(k_ref), load(v_ref)
    q1, k1, v1 = pool(q0), pool(k0), pool(v0)
    q2, k2, v2 = pool(q1), pool(k1), pool(v1)
    tasks = []
    for b in range(2):
        c = 64 * (b ^ 1)
        tasks.append((rows(q2, 64 * b, 64), rows(k2, c, 64), rows(v2, c, 64), 2))
    for p in range(4):
        c = 32 * (p ^ 1)
        tasks.append((rows(q1, 32 * p, 32), rows(k1, c, 32), rows(v1, c, 32), 1))
    for p in range(4):
        c = 32 * p
        tasks.append((rows(q0, c, 32), rows(k0, c, 32), rows(v0, c, 32), 0))
    done = attend_all(tasks)
    at2, at1, at0 = done[:2], done[2:6], done[6:]

    lane = lax.broadcasted_iota(jnp.int32, (128, WIDTH), 1)
    lses = [[None] * 4 for _ in range(8)]
    for p in range(4):
        off = 32 * (p % 2)
        for j in range(4):
            i = j // 2
            one = tuple(x[32 * j : 32 * j + 32] for x in at1[p])
            two = tuple(x[64 * i + off : 64 * i + off + 32] for x in at2[p // 2])
            coarse = merge(one, two)
            for k in (2 * j, 2 * j + 1):
                m, s, n = merge(tuple(x[32 * k : 32 * k + 32] for x in at0[p]), coarse)
                o_ref[128 * k + 32 * p : 128 * k + 32 * p + 32, :] = n / s
                lses[k][p] = m + jnp.log2(s)
    for k in range(8):
        old = lse_ref[128 * k : 128 * k + 128, :]
        lse_ref[128 * k : 128 * k + 128, :] = jnp.where(lane == head, jnp.concatenate(lses[k], axis=0), old)


def local_call(q, k, v, first, count):
    block = pl.BlockSpec((ROWS, WIDTH), lambda h: (0, h + first))
    return pl.pallas_call(
        functools.partial(local_body, first),
        name="local_levels",
        grid=(count,),
        in_specs=[block] * 3,
        out_specs=[pl.BlockSpec((ROWS, WIDTH), lambda h: (0, h)), pl.BlockSpec((ROWS, WIDTH), lambda h: (0, 0))],
        out_shape=[
            pltpu.HBM((ROWS, count * WIDTH), F32),
            pltpu.HBM((ROWS, WIDTH), F32),
        ],
        compiler_params=params(16),
        cost_estimate=pl.CostEstimate(
            flops=(count << 30), bytes_accessed=count << 21, transcendentals=count << 19
        ),
    )(in_hbm(q), in_hbm(k), in_hbm(v))


def near_body(q3_ref, mean_ref, half_ref, kv4a_ref, kv4b_ref, o_ref, lse_ref, scratch, *, step):
    group = pl.program_id(0)
    lane = lax.broadcasted_iota(jnp.int32, (128, WIDTH), 1)
    tasks = []
    for h in range(step):
        cols = slice(WIDTH * h, WIDTH * h + WIDTH)
        scratch[h, 0, :, :] = q3_ref[:, cols]
        q4 = 0.5 * (scratch[h, 0, pl.ds(0, 64, stride=2), :] + scratch[h, 0, pl.ds(1, 64, stride=2), :])
        k4 = jnp.concatenate([kv4a_ref[0, :, cols], kv4b_ref[0, :, cols]], axis=0)
        v4 = jnp.concatenate([kv4a_ref[1, :, cols], kv4b_ref[1, :, cols]], axis=0)
        tasks.append((q4, k4, v4, 4))
        k3, v3 = (
            jnp.concatenate(
                [mean_ref[i, :, cols] + half_ref[i, :, cols], mean_ref[i, :, cols] - half_ref[i, :, cols]], axis=0
            )
            for i in range(2)
        )
        tasks.append((q3_ref[:, cols], k3, v3, 3))
    done = attend_all(tasks)
    packed = lse_ref[...]
    for h in range(step):
        cols = slice(WIDTH * h, WIDTH * h + WIDTH)
        for i, x in enumerate(done[2 * h]):
            x = jnp.broadcast_to(x, (64, WIDTH))
            scratch[h, i + 1, pl.ds(0, 64, stride=2), :] = x
            scratch[h, i + 1, pl.ds(1, 64, stride=2), :] = x
        m, s, n = merge(done[2 * h + 1], (scratch[h, 1], scratch[h, 2], scratch[h, 3]))
        o_ref[:, cols] = n / s
        packed = jnp.where(lane == group * step + h, m + jnp.log2(s), packed)
    lse_ref[...] = packed


def near_call(q3, mean, half, kv4a, kv4b):
    step = 8
    wide = step * WIDTH
    return pl.pallas_call(
        functools.partial(near_body, step=step),
        name="near_levels",
        grid=(HEADS // step,),
        in_specs=[
            pl.BlockSpec((128, wide), lambda h: (0, h)),
        ]
        + [pl.BlockSpec((2, 64, wide), lambda h: (0, 0, h))] * 4,
        out_specs=[pl.BlockSpec((128, wide), lambda h: (0, h)), pl.BlockSpec((128, WIDTH), lambda h: (0, 0))],
        out_shape=[
            pltpu.HBM((128, HEADS * WIDTH), F32),
            pltpu.HBM((128, WIDTH), F32),
        ],
        scratch_shapes=[pltpu.VMEM((step, 4, 128, WIDTH), F32)],
        compiler_params=params(),
        cost_estimate=pl.CostEstimate(flops=400 << 20, bytes_accessed=4 << 20, transcendentals=1 << 18),
    )(in_hbm(q3), mean, half, kv4a, kv4b)


def rise_body(got_ref, a6_ref, a7_ref, a8_ref, a9_ref, scratch):
    outs = (a6_ref, a7_ref, a8_ref, a9_ref)
    for i in range(2):
        for s in range(8):
            scratch[32 * s : 32 * s + 32, :] = got_ref[s, 32 * (i + 1) : 32 * (i + 2), :]
        count, base = 128, 0
        for ref in outs:
            x = 0.5 * (
                scratch[pl.ds(base, count, stride=2), :] + scratch[pl.ds(base + 1, count, stride=2), :]
            )
            ref[i] = x
            base = base + 2 * count
            if count > 16:
                scratch[base : base + count, :] = x
            count = count // 2


def rise_call(got):
    return pl.pallas_call(
        rise_body,
        name="rise_rows",
        out_shape=[jax.ShapeDtypeStruct((2, n, WIDTH), F32) for n in (128, 64, 32, 16)],
        scratch_shapes=[pltpu.VMEM((512, WIDTH), F32)],
        compiler_params=params(),
        cost_estimate=pl.CostEstimate(flops=1 << 18, bytes_accessed=1 << 19, transcendentals=0),
    )(got)


def far_body(got_ref, kv6_ref, near_ref, across_ref, out_ref, qs, es):
    q5 = jnp.concatenate([got_ref[s, 0:32, :] for s in range(8)], axis=0)
    qs[0:256, :] = q5
    base, count = 0, 128
    queries = [q5]
    while count >= 16:
        x = 0.5 * (qs[pl.ds(base, count, stride=2), :] + qs[pl.ds(base + 1, count, stride=2), :])
        queries.append(x)
        base = base + 2 * count
        if count > 16:
            qs[base : base + count, :] = x
        count = count // 2

    def keys(i, first, count):
        return jnp.concatenate([near_ref[i, first : first + count], across_ref[i, first : first + count]], axis=0)

    tasks = []
    for g in range(2):
        other = range(4) if g == 1 else range(4, 8)
        k5 = jnp.concatenate([got_ref[s, 32:64, :] for s in other], axis=0)
        v5 = jnp.concatenate([got_ref[s, 64:96, :] for s in other], axis=0)
        tasks.append((q5[128 * g : 128 * g + 128], k5, v5, 5))
    tasks.append((queries[1], kv6_ref[0], kv6_ref[1], 6))
    for i in range(3):
        tasks.append((queries[2 + i], keys(0, 64 * i, 64), keys(1, 64 * i, 64), 7 + i))
    done = attend_all(tasks)
    five = tuple(jnp.concatenate([a, b], axis=0) for a, b in zip(done[0], done[1]))
    levels = [five] + done[2:]
    running = levels[-1]
    base = 0
    for finer in reversed(levels[:-1]):
        n = running[0].shape[0]
        wide = []
        for i, x in enumerate(running):
            x = jnp.broadcast_to(x, (n, WIDTH))
            es[i, pl.ds(base, n, stride=2), :] = x
            es[i, pl.ds(base + 1, n, stride=2), :] = x
            wide.append(es[i, base : base + 2 * n, :])
        base = base + 2 * n
        running = merge(finer, tuple(wide))
    m, s, n = running
    o = n / s
    lse = jnp.broadcast_to(m + jnp.log2(s), (256, WIDTH))
    for d in range(8):
        out_ref[d, 0:32, :] = o[32 * d : 32 * d + 32]
        out_ref[d, 32:64, :] = lse[32 * d : 32 * d + 32]


def far_call(got, kv6, near, across):
    return pl.pallas_call(
        far_body,
        name="far_levels",
        out_shape=pltpu.HBM((HEADS, 64, WIDTH), F32),
        scratch_shapes=[pltpu.VMEM((512, WIDTH), F32), pltpu.VMEM((3, 512, WIDTH), F32)],
        compiler_params=params(),
        cost_estimate=pl.CostEstimate(flops=100 << 20, bytes_accessed=1 << 20, transcendentals=1 << 17),
    )(got, kv6, near, across)


def join_body(*refs):
    n = len(CALLS)
    own_hbm, own_lse_hbm = refs[:n], refs[n : 2 * n]
    o34_hbm, lse34_hbm, far_ref, out_hbm = refs[2 * n : 2 * n + 4]
    own, own_lse, o34, lse34, wide, stage, own_sems, sems, out_sems = refs[2 * n + 4 :]
    place = [(c, i) for c, count in enumerate(CALLS) for i in range(count)]

    def columns(h):
        return slice(WIDTH * h, WIDTH * h + WIDTH)

    def fetch(h):
        c, i = place[h]
        return pltpu.make_async_copy(own_hbm[c].at[:, columns(i)], own.at[h], own_sems.at[h])

    def send(h):
        return pltpu.make_async_copy(stage.at[h % 4], out_hbm.at[:, columns(h)], out_sems.at[h % 4])

    others = [
        pltpu.make_async_copy(source, target, sems.at[i])
        for i, (source, target) in enumerate(
            [(lse34_hbm, lse34), (o34_hbm, o34)] + [(own_lse_hbm[c], own_lse.at[c]) for c in range(n)]
        )
    ]
    for copy in others[:3]:
        copy.start()
    for h in range(HEADS):
        fetch(h).start()
        if h == 0:
            for copy in others[3:]:
                copy.start()
    for copy in others:
        copy.wait()

    def column(x, h):
        return jnp.broadcast_to(x[:, h : h + 1], (128, WIDTH))

    for h in range(HEADS):
        if h >= 4:
            send(h - 4).wait()
        for i in range(2):
            x = far_ref[h, 32 * i : 32 * i + 32, :]
            for c in range(4):
                wide[h % 2, i, pl.ds(c, 32, stride=4), :] = x
        coarse = merge((column(lse34[...], h), 1.0, o34[:, columns(h)]), (wide[h % 2, 1], 1.0, wide[h % 2, 0]))
        fetch(h).wait()
        for k in range(8):
            part = slice(128 * k, 128 * k + 128)
            lse = column(own_lse[place[h][0], part, :], h)
            _, den, num = merge((lse, 1.0, own[h, part, :]), coarse)
            stage[h % 4, pl.ds(k, 128, stride=8), :] = num / den
        send(h).start()
    for h in range(HEADS - 4, HEADS):
        send(h).wait()


def join_call(own, o34, lse34, far):
    n = len(CALLS)
    anywhere = pl.BlockSpec(memory_space=pl.ANY)
    return pl.pallas_call(
        join_body,
        name="join_levels",
        in_specs=[anywhere] * (2 * n + 2) + [pl.BlockSpec(memory_space=pltpu.VMEM)],
        out_specs=anywhere,
        out_shape=pltpu.HBM((ROWS, HEADS * WIDTH), F32),
        scratch_shapes=[
            pltpu.VMEM((HEADS, ROWS, WIDTH), F32),
            pltpu.VMEM((n, ROWS, WIDTH), F32),
            pltpu.VMEM((128, HEADS * WIDTH), F32),
            pltpu.VMEM((128, WIDTH), F32),
            pltpu.VMEM((2, 2, 128, WIDTH), F32),
            pltpu.VMEM((4, ROWS, WIDTH), F32),
            pltpu.SemaphoreType.DMA((HEADS,)),
            pltpu.SemaphoreType.DMA((n + 2,)),
            pltpu.SemaphoreType.DMA((4,)),
        ],
        compiler_params=params(16),
        cost_estimate=pl.CostEstimate(flops=16 << 20, bytes_accessed=9 << 20, transcendentals=1 << 20),
    )(*[in_hbm(o) for o, _ in own], *[in_hbm(lse) for _, lse in own], in_hbm(o34), in_hbm(lse34), far)


def hop(x, axis, flip):
    return lax.ppermute(x, axis, [(i, i ^ flip) for i in range(lax.axis_size(axis))])


def transpose_heads(x):
    return lax.all_to_all(x, "node", 0, 0, axis_index_groups=GROUPS, tiled=True)


def on_device(queries, keys, values):
    q3, mean, half, pay = pool_call(queries, keys, values)
    got = transpose_heads(pay)
    one = local_call(queries, keys, values, 0, CALLS[0])
    mean, half, one, queries = lax.optimization_barrier((mean, half, one, queries))
    mean3 = hop(mean, "node", 1)
    kv4a = hop(mean, "node", 3)
    two = local_call(queries, keys, values, CALLS[0], CALLS[1])
    got, two = lax.optimization_barrier((got, two))
    a6, a7, a8, a9 = rise_call(got)

    kv6 = hop(a6, "node", 12)
    c7 = hop(a7, "seq", 1)
    r8 = hop(a8, "seq", 2)
    r9a = hop(a9, "seq", 4)
    r9b = hop(a9, "seq", 6)
    fetched = jnp.concatenate([r8, r9a, r9b], axis=1)
    fetched, kv6, mean3, kv4a, half = lax.optimization_barrier((fetched, kv6, mean3, kv4a, half))
    half3 = hop(half, "node", 1)
    kv4b = hop(mean3, "node", 3)
    passed = hop(fetched, "seq", 1)
    near = jnp.concatenate([c7, fetched[:, :32], passed[:, :32], fetched[:, 32:], passed[:, 32:]], axis=1)
    across = hop(near, "node", 12)

    far = far_call(got, kv6, near, across)
    back = transpose_heads(far)
    queries, keys, values, far = lax.optimization_barrier((queries, keys, values, far))
    three = local_call(queries, keys, values, CALLS[0] + CALLS[1], CALLS[2])
    o34, lse34 = near_call(q3, mean3, half3, kv4a, kv4b)
    return join_call([one, two, three], o34, lse34, back)


def solution(mesh):
    spec = P(("seq", "node"), None)
    return jax.shard_map(on_device, mesh=mesh, in_specs=(spec, spec, spec), out_specs=spec, check_vma=False)
```

```python
import functools
import math

import jax
import jax.numpy as jnp
from jax import lax
from jax.experimental import pallas as pl
from jax.experimental.pallas import tpu as pltpu
from jax.sharding import PartitionSpec as P

HEADS = 8
PACK = 208
BACK = 72
CALLS = (4, 2, 2)
WIDTH = 128
ROWS = 1024
F32 = jnp.float32
BF16 = jnp.bfloat16
SCALE = WIDTH ** (-0.5) / math.log(2.0)
MIB = 1024 * 1024

GROUPS = [list(range(8)), [12, 13, 14, 15, 8, 9, 10, 11]]


def params(mib=12):
    return pltpu.CompilerParams(vmem_limit_bytes=mib * MIB)


def in_hbm(x):
    return pltpu.with_memory_space_constraint(x, pltpu.HBM)


def split(x):
    hi = x.astype(BF16)
    lo = (x - hi.astype(F32)).astype(BF16)
    return hi, lo


def dot_nt(a, b):
    return lax.dot_general(a, b, (((1,), (1,)), ((), ())), preferred_element_type=F32)


def dot_nn(a, b):
    return lax.dot_general(a, b, (((1,), (0,)), ((), ())), preferred_element_type=F32)


def key_side(k):
    hi, lo = split(k)
    return jnp.concatenate([hi, hi], axis=1), jnp.concatenate([lo, jnp.zeros_like(lo)], axis=1)


def scores(q, sides):
    hi, lo = split(q)
    both = jnp.concatenate([hi, lo], axis=1)
    first, second = sides
    n = first.shape[0]
    if n == 128:
        s = dot_nt(both, jnp.concatenate([first, second], axis=0))
        return s[:, :n] + s[:, n:]
    return dot_nt(both, first) + dot_nt(both, second)


def weigh(p, side):
    hi, lo = side
    p_hi, p_lo = split(p)
    if hi.shape[0] == 128:
        left = jnp.concatenate([p_hi, p_lo], axis=1)
        right = jnp.concatenate(
            [jnp.concatenate([hi, lo], axis=1), jnp.concatenate([hi, jnp.zeros_like(lo)], axis=1)], axis=0
        )
        r = dot_nn(left, right)
        return r[:, :WIDTH] + r[:, WIDTH:]
    r = dot_nn(p_hi, jnp.concatenate([hi, lo], axis=1))
    return r[:, :WIDTH] + r[:, WIDTH:] + dot_nn(p_lo, hi)


def attend_all(tasks):
    grids = [scores(q, key_side(k)) for q, k, _, _ in tasks]
    peaks = [jnp.max(s, axis=1, keepdims=True) for s in grids]
    weights = [jnp.exp2(s - peak) for s, peak in zip(grids, peaks)]
    totals = [jnp.sum(p, axis=1, keepdims=True) for p in weights]
    numerators = [weigh(p, split(task[2])) for p, task in zip(weights, tasks)]
    return [(peak + float(task[3]), t, n) for peak, t, n, task in zip(peaks, totals, numerators, tasks)]


def merge(a, b):
    ma, sa, na = a
    mb, sb, nb = b
    m = jnp.maximum(ma, mb)
    fa, fb = jnp.exp2(ma - m), jnp.exp2(mb - m)
    return m, sa * fa + sb * fb, na * fa + nb * fb


def pool_eight(ref):
    total = ref[pl.ds(0, 128, stride=8), :]
    for k in range(1, 8):
        total = total + ref[pl.ds(k, 128, stride=8), :]
    return total


def pool_pairs(ref, n):
    return 0.5 * (ref[pl.ds(0, n, stride=2), :] + ref[pl.ds(1, n, stride=2), :])


def pool_kv_body(k_hbm, v_hbm, k3_hbm, v3_hbm, pay_hbm, x8_ref, x9_ref, rows, three, four, more, sems, sems3, sems4):
    arrays, outs = (k_hbm, v_hbm), (k3_hbm, v3_hbm)

    def cols(h):
        return slice(WIDTH * h, WIDTH * h + WIDTH)

    def fetch(i, h):
        return pltpu.make_async_copy(arrays[i].at[:, cols(h)], rows.at[i, h], sems.at[i, h])

    def send3(i, h):
        return pltpu.make_async_copy(three.at[i, h], outs[i].at[:, cols(h)], sems3.at[i, h])

    def send4(i, h):
        return pltpu.make_async_copy(four.at[i, h], pay_hbm.at[h, 64 * i + 64 : 64 * i + 128, :], sems4.at[i, h])

    every = [(i, h) for h in range(HEADS) for i in range(2)]
    for i, h in every:
        fetch(i, h).start()
    for i, h in every:
        fetch(i, h).wait()
        three[i, h] = 0.125 * pool_eight(rows.at[i, h])
        send3(i, h).start()
        four[i, h] = pool_pairs(three.at[i, h], 64)
        send4(i, h).start()
        x7 = four[i, h, pl.ds(0, 8, stride=8), :]
        for k in range(1, 8):
            x7 = x7 + four[i, h, pl.ds(k, 8, stride=8), :]
        more[i] = 0.125 * x7
        x8 = pool_pairs(more.at[i], 4)
        x8_ref[h, 4 * i : 4 * i + 4, :] = x8
        x9_ref[h, 2 * i : 2 * i + 2, :] = jnp.concatenate(
            [0.5 * (x8[0:1] + x8[1:2]), 0.5 * (x8[2:3] + x8[3:4])], axis=0
        )
    for i, h in every:
        send3(i, h).wait()
        send4(i, h).wait()


def pool_kv_call(k, v):
    anywhere = pl.BlockSpec(memory_space=pl.ANY)
    vmem = pl.BlockSpec(memory_space=pltpu.VMEM)
    return pl.pallas_call(
        pool_kv_body,
        name="pool_keys",
        in_specs=[anywhere] * 2,
        out_specs=[anywhere] * 3 + [vmem] * 2,
        out_shape=[
            pltpu.HBM((128, HEADS * WIDTH), F32),
            pltpu.HBM((128, HEADS * WIDTH), F32),
            pltpu.HBM((HEADS, PACK, WIDTH), F32),
            jax.ShapeDtypeStruct((HEADS, 8, WIDTH), F32),
            jax.ShapeDtypeStruct((HEADS, 4, WIDTH), F32),
        ],
        scratch_shapes=[
            pltpu.VMEM((2, HEADS, ROWS, WIDTH), F32),
            pltpu.VMEM((2, HEADS, 128, WIDTH), F32),
            pltpu.VMEM((2, HEADS, 64, WIDTH), F32),
            pltpu.VMEM((2, 8, WIDTH), F32),
            pltpu.SemaphoreType.DMA((2, HEADS)),
            pltpu.SemaphoreType.DMA((2, HEADS)),
            pltpu.SemaphoreType.DMA((2, HEADS)),
        ],
        compiler_params=params(20),
        cost_estimate=pl.CostEstimate(flops=2 << 20, bytes_accessed=10 << 20, transcendentals=0),
    )(in_hbm(k), in_hbm(v))


def pool_q_body(q_hbm, pay_in, q3_hbm, pay_hbm, rows, three, four, sems, sems3, sems4):
    def cols(h):
        return slice(WIDTH * h, WIDTH * h + WIDTH)

    def fetch(h):
        return pltpu.make_async_copy(q_hbm.at[:, cols(h)], rows.at[h], sems.at[h])

    def send3(h):
        return pltpu.make_async_copy(three.at[h], q3_hbm.at[:, cols(h)], sems3.at[h])

    def send4(h):
        return pltpu.make_async_copy(four.at[h], pay_hbm.at[h, 0:64, :], sems4.at[h])

    for h in range(HEADS):
        fetch(h).start()
    for h in range(HEADS):
        fetch(h).wait()
        three[h] = (0.125 * SCALE) * pool_eight(rows.at[h])
        send3(h).start()
        four[h] = pool_pairs(three.at[h], 64)
        send4(h).start()
    for h in range(HEADS):
        send3(h).wait()
        send4(h).wait()


def pool_q_call(q, pay):
    anywhere = pl.BlockSpec(memory_space=pl.ANY)
    return pl.pallas_call(
        pool_q_body,
        name="pool_queries",
        in_specs=[anywhere] * 2,
        out_specs=[anywhere] * 2,
        out_shape=[pltpu.HBM((128, HEADS * WIDTH), F32), pltpu.HBM((HEADS, PACK, WIDTH), F32)],
        input_output_aliases={1: 1},
        scratch_shapes=[
            pltpu.VMEM((HEADS, ROWS, WIDTH), F32),
            pltpu.VMEM((HEADS, 128, WIDTH), F32),
            pltpu.VMEM((HEADS, 64, WIDTH), F32),
            pltpu.SemaphoreType.DMA((HEADS,)),
            pltpu.SemaphoreType.DMA((HEADS,)),
            pltpu.SemaphoreType.DMA((HEADS,)),
        ],
        compiler_params=params(),
        cost_estimate=pl.CostEstimate(flops=2 << 30, bytes_accessed=5 << 20, transcendentals=0),
    )(in_hbm(q), in_hbm(pay))


def pack_body(pay_hbm, r8_ref, r9a_ref, r9b_ref, out_hbm, rows, sem):
    rows[:, 0:8, :] = r8_ref[...]
    rows[:, 8:12, :] = r9a_ref[...]
    rows[:, 12:16, :] = r9b_ref[...]
    copy = pltpu.make_async_copy(rows, out_hbm.at[:, 192:208, :], sem)
    copy.start()
    copy.wait()


def pack_call(pay, r8, r9a, r9b):
    vmem = pl.BlockSpec(memory_space=pltpu.VMEM)
    anywhere = pl.BlockSpec(memory_space=pl.ANY)
    return pl.pallas_call(
        pack_body,
        name="pack_rows",
        in_specs=[anywhere, vmem, vmem, vmem],
        out_specs=anywhere,
        out_shape=pltpu.HBM((HEADS, PACK, WIDTH), F32),
        input_output_aliases={0: 0},
        scratch_shapes=[pltpu.VMEM((HEADS, 16, WIDTH), F32), pltpu.SemaphoreType.DMA],
        compiler_params=params(4),
        cost_estimate=pl.CostEstimate(flops=0, bytes_accessed=1 << 17, transcendentals=0),
    )(in_hbm(pay), r8, r9a, r9b)


def local_body(first, q_ref, k_ref, v_ref, o_ref, lse_ref):
    head = pl.program_id(0) + first

    def load(ref):
        return [ref[pl.ds(k, 128, stride=8), :] for k in range(8)]

    def pool(parts):
        return [0.5 * (parts[2 * i] + parts[2 * i + 1]) for i in range(len(parts) // 2)]

    def rows(parts, begin, count):
        return jnp.concatenate([x[begin : begin + count] for x in parts], axis=0)

    q0 = [x * SCALE for x in load(q_ref)]
    k0, v0 = load(k_ref), load(v_ref)
    q1, k1, v1 = pool(q0), pool(k0), pool(v0)
    q2, k2, v2 = pool(q1), pool(k1), pool(v1)
    tasks = []
    for b in range(2):
        c = 64 * (b ^ 1)
        tasks.append((rows(q2, 64 * b, 64), rows(k2, c, 64), rows(v2, c, 64), 2))
    for p in range(4):
        c = 32 * (p ^ 1)
        tasks.append((rows(q1, 32 * p, 32), rows(k1, c, 32), rows(v1, c, 32), 1))
    for p in range(4):
        c = 32 * p
        tasks.append((rows(q0, c, 32), rows(k0, c, 32), rows(v0, c, 32), 0))
    done = attend_all(tasks)
    at2, at1, at0 = done[:2], done[2:6], done[6:]

    lane = lax.broadcasted_iota(jnp.int32, (128, WIDTH), 1)
    lses = [[None] * 4 for _ in range(8)]
    for p in range(4):
        off = 32 * (p % 2)
        for j in range(4):
            i = j // 2
            one = tuple(x[32 * j : 32 * j + 32] for x in at1[p])
            two = tuple(x[64 * i + off : 64 * i + off + 32] for x in at2[p // 2])
            coarse = merge(one, two)
            for k in (2 * j, 2 * j + 1):
                m, s, n = merge(tuple(x[32 * k : 32 * k + 32] for x in at0[p]), coarse)
                o_ref[128 * k + 32 * p : 128 * k + 32 * p + 32, :] = n / s
                lses[k][p] = m + jnp.log2(s)
    for k in range(8):
        old = lse_ref[128 * k : 128 * k + 128, :]
        lse_ref[128 * k : 128 * k + 128, :] = jnp.where(lane == head, jnp.concatenate(lses[k], axis=0), old)


def local_call(q, k, v, first, count):
    block = pl.BlockSpec((ROWS, WIDTH), lambda h: (0, h + first))
    return pl.pallas_call(
        functools.partial(local_body, first),
        name="local_levels",
        grid=(count,),
        in_specs=[block] * 3,
        out_specs=[pl.BlockSpec((ROWS, WIDTH), lambda h: (0, h)), pl.BlockSpec((ROWS, WIDTH), lambda h: (0, 0))],
        out_shape=[
            pltpu.HBM((ROWS, count * WIDTH), F32),
            pltpu.HBM((ROWS, WIDTH), F32),
        ],
        compiler_params=params(16),
        cost_estimate=pl.CostEstimate(
            flops=(count << 30), bytes_accessed=count << 21, transcendentals=count << 19
        ),
    )(in_hbm(q), in_hbm(k), in_hbm(v))


def rise_body(got_ref, six_ref, seven_ref, scratch):
    for i in range(2):
        for s in range(8):
            scratch[i, 64 * s : 64 * s + 64, :] = got_ref[s, 64 * (i + 1) : 64 * (i + 2), :]
            scratch[i, 640 + 4 * s : 644 + 4 * s, :] = got_ref[s, 192 + 4 * i : 196 + 4 * i, :]
            for j in range(2):
                begin = 200 + 4 * j + 2 * i
                place = 672 + 16 * j + 2 * s
                scratch[i, place : place + 2, :] = got_ref[s, begin : begin + 2, :]
        x6 = scratch[i, pl.ds(0, 128, stride=4), :]
        for k in range(1, 4):
            x6 = x6 + scratch[i, pl.ds(k, 128, stride=4), :]
        x6 = 0.25 * x6
        scratch[i, 512:640, :] = x6
        six_ref[i, 0:128, :] = x6
        seven_ref[i, 0:64, :] = 0.5 * (
            scratch[i, pl.ds(512, 64, stride=2), :] + scratch[i, pl.ds(513, 64, stride=2), :]
        )
        six_ref[i, 128:192, :] = scratch[i, 640:704, :]
        seven_ref[i, 64:128, :] = scratch[i, 640:704, :]


def rise_call(got):
    return pl.pallas_call(
        rise_body,
        name="rise_rows",
        out_shape=[jax.ShapeDtypeStruct((2, n, WIDTH), F32) for n in (192, 128)],
        scratch_shapes=[pltpu.VMEM((2, 704, WIDTH), F32)],
        compiler_params=params(),
        cost_estimate=pl.CostEstimate(flops=1 << 18, bytes_accessed=1 << 19, transcendentals=0),
    )(got)


def far_body(got_ref, here_ref, six_ref, core_ref, seven_ref, out_ref, scratch, es):
    def gather(i, sources):
        return jnp.concatenate([got_ref[s, 64 * i : 64 * i + 64, :] for s in sources], axis=0)

    def halve(i, base, count):
        return 0.5 * (scratch[i, pl.ds(base, count, stride=2), :] + scratch[i, pl.ds(base + 1, count, stride=2), :])

    for i in range(3):
        scratch[i, 0:512, :] = gather(i, range(8))
        base, count = 0, 256
        while count >= (16 if i == 0 else 256):
            x = halve(i, base, count)
            base = base + 2 * count
            scratch[i, base : base + count, :] = x
            count = count // 2

    def sibling(i, level):
        if level == 6:
            return six_ref[i, 0:128, :]
        if level == 7:
            return jnp.concatenate([core_ref[i, 0:64, :], seven_ref[i, 0:64, :]], axis=0)
        low = 64 + 32 * (level - 8)
        return jnp.concatenate(
            [
                here_ref[i, 64 + low : 96 + low, :],
                core_ref[i, low : low + 32, :],
                six_ref[i, 64 + low : 96 + low, :],
                seven_ref[i, low : low + 32, :],
            ],
            axis=0,
        )

    tasks = []
    for level, base, blocks in ((4, 0, 4), (5, 512, 2)):
        for g in range(blocks):
            mine = slice(base + 128 * g, base + 128 * g + 128)
            other = slice(base + 128 * (g ^ 1), base + 128 * (g ^ 1) + 128)
            tasks.append((scratch[0, mine, :], scratch[1, other, :], scratch[2, other, :], level))
    base, count = 768, 128
    for level in range(6, 10):
        tasks.append((scratch[0, base : base + count, :], sibling(0, level), sibling(1, level), level))
        base, count = base + count, count // 2
    done = attend_all(tasks)
    levels = []
    for few in (done[0:4], done[4:6]):
        levels.append(tuple(jnp.concatenate(x, axis=0) for x in zip(*few)))
    levels.extend(done[6:])
    running = levels[-1]
    base = 0
    for finer in reversed(levels[:-1]):
        n = running[0].shape[0]
        wide = []
        for i, x in enumerate(running):
            x = jnp.broadcast_to(x, (n, WIDTH))
            es[i, pl.ds(base, n, stride=2), :] = x
            es[i, pl.ds(base + 1, n, stride=2), :] = x
            wide.append(es[i, base : base + 2 * n, :])
        base = base + 2 * n
        running = merge(finer, tuple(wide))
    m, s, n = running
    o = n / s
    lse = jnp.broadcast_to(m + jnp.log2(s), (512, WIDTH))
    for g in range(4):
        row = jnp.transpose(lse[128 * g : 128 * g + 128])[0:8]
        for d in range(2):
            out_ref[2 * g + d, 0:64, :] = o[128 * g + 64 * d : 128 * g + 64 * d + 64]
            out_ref[2 * g + d, 64:72, :] = row if d == 0 else pltpu.roll(row, 64, 1)


def far_call(got, here, six, core, seven):
    return pl.pallas_call(
        far_body,
        name="far_levels",
        out_shape=pltpu.HBM((HEADS, BACK, WIDTH), F32),
        scratch_shapes=[pltpu.VMEM((3, 1024, WIDTH), F32), pltpu.VMEM((3, 1024, WIDTH), F32)],
        compiler_params=params(),
        cost_estimate=pl.CostEstimate(flops=100 << 20, bytes_accessed=1 << 20, transcendentals=1 << 17),
    )(got, here, six, core, seven)


def near_body(q3_ref, k3_ref, v3_ref, o_ref, lse_ref):
    lane = lax.broadcasted_iota(jnp.int32, (128, WIDTH), 1)
    packed = jnp.zeros((128, WIDTH), F32)
    cols = [slice(WIDTH * h, WIDTH * h + WIDTH) for h in range(HEADS)]
    done = attend_all([(q3_ref[:, c], k3_ref[:, c], v3_ref[:, c], 3) for c in cols])
    for h, (m, s, n) in enumerate(done):
        o_ref[:, cols[h]] = n / s
        packed = jnp.where(lane == h, m + jnp.log2(s), packed)
    lse_ref[...] = packed


def near_call(q3, k3, v3):
    return pl.pallas_call(
        near_body,
        name="near_level",
        out_shape=[pltpu.HBM((128, HEADS * WIDTH), F32), pltpu.HBM((128, WIDTH), F32)],
        compiler_params=params(),
        cost_estimate=pl.CostEstimate(flops=200 << 20, bytes_accessed=2 << 20, transcendentals=1 << 17),
    )(in_hbm(q3), k3, v3)


def share(a, b):
    return 1.0 / (1.0 + jnp.exp2(b - a))


def join_body(*refs):
    n = len(CALLS)
    own_hbm, own_lse_hbm = refs[:n], refs[n : 2 * n]
    o3_hbm, lse3_hbm, far_ref, out_hbm = refs[2 * n : 2 * n + 4]
    own, own_lse, o3, lse3, wide, stage, own_sems, sems, out_sems = refs[2 * n + 4 :]
    place = [(c, i) for c, count in enumerate(CALLS) for i in range(count)]

    def columns(h):
        return slice(WIDTH * h, WIDTH * h + WIDTH)

    def fetch(h):
        c, i = place[h]
        return pltpu.make_async_copy(own_hbm[c].at[:, columns(i)], own.at[h], own_sems.at[h])

    def send(h):
        return pltpu.make_async_copy(stage.at[h % 4], out_hbm.at[:, columns(h)], out_sems.at[h % 4])

    fetch(0).start()
    others = [pltpu.make_async_copy(lse3_hbm, lse3, sems.at[0]), pltpu.make_async_copy(o3_hbm, o3, sems.at[1])]
    others += [pltpu.make_async_copy(own_lse_hbm[c], own_lse.at[c], sems.at[c + 2]) for c in range(n)]
    for copy in others:
        copy.start()
    for h in range(1, HEADS):
        fetch(h).start()
    for copy in others:
        copy.wait()

    for h in range(HEADS):
        lse = jnp.transpose(jnp.broadcast_to(far_ref[h, 64:65, :], (128, WIDTH)))[0:64]
        for i, x in enumerate((far_ref[h, 0:64, :], lse)):
            for c in range(2):
                wide[h % 2, i, pl.ds(c, 64, stride=2), :] = x
        far_o, far_lse = wide[h % 2, 0], wide[h % 2, 1]
        near_lse = jnp.broadcast_to(lse3[:, h : h + 1], (128, WIDTH))
        top = jnp.maximum(far_lse, near_lse)
        rest_lse = top + jnp.log2(jnp.exp2(far_lse - top) + jnp.exp2(near_lse - top))
        rest = far_o + (o3[:, columns(h)] - far_o) * share(near_lse, far_lse)
        fetch(h).wait()
        if h >= 4:
            send(h - 4).wait()
        for k in range(8):
            part = slice(128 * k, 128 * k + 128)
            lse = jnp.broadcast_to(own_lse[place[h][0], part, h : h + 1], (128, WIDTH))
            stage[h % 4, pl.ds(k, 128, stride=8), :] = rest + (own[h, part, :] - rest) * share(lse, rest_lse)
        send(h).start()
    for h in range(HEADS - 4, HEADS):
        send(h).wait()


def join_call(own, o3, lse3, far):
    n = len(CALLS)
    anywhere = pl.BlockSpec(memory_space=pl.ANY)
    return pl.pallas_call(
        join_body,
        name="join_levels",
        in_specs=[anywhere] * (2 * n + 2) + [pl.BlockSpec(memory_space=pltpu.VMEM)],
        out_specs=anywhere,
        out_shape=pltpu.HBM((ROWS, HEADS * WIDTH), F32),
        scratch_shapes=[
            pltpu.VMEM((HEADS, ROWS, WIDTH), F32),
            pltpu.VMEM((n, ROWS, WIDTH), F32),
            pltpu.VMEM((128, HEADS * WIDTH), F32),
            pltpu.VMEM((128, WIDTH), F32),
            pltpu.VMEM((2, 2, 128, WIDTH), F32),
            pltpu.VMEM((4, ROWS, WIDTH), F32),
            pltpu.SemaphoreType.DMA((HEADS,)),
            pltpu.SemaphoreType.DMA((n + 2,)),
            pltpu.SemaphoreType.DMA((4,)),
        ],
        compiler_params=params(20),
        cost_estimate=pl.CostEstimate(flops=16 << 20, bytes_accessed=9 << 20, transcendentals=1 << 20),
    )(*[in_hbm(o) for o, _ in own], *[in_hbm(lse) for _, lse in own], in_hbm(o3), in_hbm(lse3), far)


def hop(x, axis, flip):
    return lax.ppermute(x, axis, [(i, i ^ flip) for i in range(lax.axis_size(axis))])


def transpose_heads(x):
    return lax.all_to_all(x, "node", 0, 0, axis_index_groups=GROUPS, tiled=True)


def on_device(queries, keys, values):
    k3, v3, pay, x8, x9 = pool_kv_call(keys, values)
    first = [sum(CALLS[:i]) for i in range(len(CALLS))]
    local = []

    def local_part(i, *after):
        q, k, v = lax.optimization_barrier((queries, keys, values) + after)[:3]
        return local_call(q, k, v, first[i], CALLS[i])

    r8, r9a, r9b = hop(x8, "seq", 2), hop(x9, "seq", 4), hop(x9, "seq", 6)
    q3, pay = pool_q_call(queries, pay)
    pay = pack_call(pay, r8, r9a, r9b)
    got = transpose_heads(pay)
    part = local_part(0, pay)
    got, part = lax.optimization_barrier((got, part))
    local.append(part)
    _, k3, v3 = lax.optimization_barrier((part, k3, v3))
    sib_k3, sib_v3 = hop(k3, "node", 1), hop(v3, "node", 1)

    here6, here7 = rise_call(got)
    six = hop(here6, "node", 12)
    core = hop(here7, "seq", 1)
    seven = hop(core, "node", 12)
    part = local_part(1, core)
    six, seven, part = lax.optimization_barrier((six, seven, part))
    local.append(part)

    far = far_call(got, here6, six, core, seven)
    back = transpose_heads(far)
    local.append(local_part(2, far))
    o3, lse3 = near_call(q3, sib_k3, sib_v3)
    return join_call(local, o3, lse3, back)


def solution(mesh):
    spec = P(("seq", "node"), None)
    return jax.shard_map(on_device, mesh=mesh, in_specs=(spec, spec, spec), out_specs=spec, check_vma=False)
```

```python
import functools
import math

import jax
import jax.numpy as jnp
from jax import lax
from jax.experimental import pallas as pl
from jax.experimental.pallas import tpu as pltpu
from jax.sharding import PartitionSpec as P

HEADS = 8
PACK = 208
BACK = 72
CALLS = (5, 2, 1)
WIDTH = 128
ROWS = 1024
F32 = jnp.float32
BF16 = jnp.bfloat16
SCALE = WIDTH ** (-0.5) / math.log(2.0)
MIB = 1024 * 1024

GROUPS = [list(range(8)), [12, 13, 14, 15, 8, 9, 10, 11]]


def params(mib=12):
    return pltpu.CompilerParams(vmem_limit_bytes=mib * MIB)


def in_hbm(x):
    return pltpu.with_memory_space_constraint(x, pltpu.HBM)


def split(x):
    hi = x.astype(BF16)
    lo = (x - hi.astype(F32)).astype(BF16)
    return hi, lo


def dot_nt(a, b):
    return lax.dot_general(a, b, (((1,), (1,)), ((), ())), preferred_element_type=F32)


def dot_nn(a, b):
    return lax.dot_general(a, b, (((1,), (0,)), ((), ())), preferred_element_type=F32)


def key_side(k):
    hi, lo = split(k)
    return jnp.concatenate([hi, hi], axis=1), jnp.concatenate([lo, jnp.zeros_like(lo)], axis=1)


def scores(q, sides):
    hi, lo = split(q)
    both = jnp.concatenate([hi, lo], axis=1)
    first, second = sides
    n = first.shape[0]
    if n == 128:
        s = dot_nt(both, jnp.concatenate([first, second], axis=0))
        return s[:, :n] + s[:, n:]
    return dot_nt(both, first) + dot_nt(both, second)


def weigh(p, side):
    hi, lo = side
    p_hi, p_lo = split(p)
    if hi.shape[0] == 128:
        left = jnp.concatenate([p_hi, p_lo], axis=1)
        right = jnp.concatenate(
            [jnp.concatenate([hi, lo], axis=1), jnp.concatenate([hi, jnp.zeros_like(lo)], axis=1)], axis=0
        )
        r = dot_nn(left, right)
        return r[:, :WIDTH] + r[:, WIDTH:]
    r = dot_nn(p_hi, jnp.concatenate([hi, lo], axis=1))
    return r[:, :WIDTH] + r[:, WIDTH:] + dot_nn(p_lo, hi)


def attend_all(tasks):
    grids = [scores(q, key_side(k)) for q, k, _, _ in tasks]
    peaks = [jnp.max(s, axis=1, keepdims=True) for s in grids]
    weights = [jnp.exp2(s - peak) for s, peak in zip(grids, peaks)]
    totals = [jnp.sum(p, axis=1, keepdims=True) for p in weights]
    numerators = [weigh(p, split(task[2])) for p, task in zip(weights, tasks)]
    return [(peak + float(task[3]), t, n) for peak, t, n, task in zip(peaks, totals, numerators, tasks)]


def merge(a, b):
    ma, sa, na = a
    mb, sb, nb = b
    m = jnp.maximum(ma, mb)
    fa, fb = jnp.exp2(ma - m), jnp.exp2(mb - m)
    return m, sa * fa + sb * fb, na * fa + nb * fb


def share(a, b):
    return 1.0 / (1.0 + jnp.exp2(b - a))


def pool_eight(ref):
    total = ref[pl.ds(0, 128, stride=8), :]
    for k in range(1, 8):
        total = total + ref[pl.ds(k, 128, stride=8), :]
    return total


def pool_pairs(ref, n):
    return 0.5 * (ref[pl.ds(0, n, stride=2), :] + ref[pl.ds(1, n, stride=2), :])


def pool_kv_body(k_hbm, v_hbm, k3_hbm, v3_hbm, pay_hbm, x8_ref, x9_ref, rows, three, four, more, sems, sems3, sems4):
    arrays, outs = (k_hbm, v_hbm), (k3_hbm, v3_hbm)

    def cols(h):
        return slice(WIDTH * h, WIDTH * h + WIDTH)

    def fetch(i, h):
        return pltpu.make_async_copy(arrays[i].at[:, cols(h)], rows.at[i, h], sems.at[i, h])

    def send3(i, h):
        return pltpu.make_async_copy(three.at[i, h], outs[i].at[:, cols(h)], sems3.at[i, h])

    def send4(i, h):
        return pltpu.make_async_copy(four.at[i, h], pay_hbm.at[h, 64 * i + 64 : 64 * i + 128, :], sems4.at[i, h])

    every = [(i, h) for h in range(HEADS) for i in range(2)]
    for i, h in every:
        fetch(i, h).start()
    for i, h in every:
        fetch(i, h).wait()
        three[i, h] = 0.125 * pool_eight(rows.at[i, h])
        send3(i, h).start()
        four[i, h] = pool_pairs(three.at[i, h], 64)
        send4(i, h).start()
        x7 = four[i, h, pl.ds(0, 8, stride=8), :]
        for k in range(1, 8):
            x7 = x7 + four[i, h, pl.ds(k, 8, stride=8), :]
        more[i] = 0.125 * x7
        x8 = pool_pairs(more.at[i], 4)
        x8_ref[h, 4 * i : 4 * i + 4, :] = x8
        x9_ref[h, 2 * i : 2 * i + 2, :] = jnp.concatenate(
            [0.5 * (x8[0:1] + x8[1:2]), 0.5 * (x8[2:3] + x8[3:4])], axis=0
        )
    for i, h in every:
        send3(i, h).wait()
        send4(i, h).wait()


def pool_kv_call(k, v):
    anywhere = pl.BlockSpec(memory_space=pl.ANY)
    vmem = pl.BlockSpec(memory_space=pltpu.VMEM)
    return pl.pallas_call(
        pool_kv_body,
        name="pool_keys",
        in_specs=[anywhere] * 2,
        out_specs=[anywhere] * 3 + [vmem] * 2,
        out_shape=[
            pltpu.HBM((128, HEADS * WIDTH), F32),
            pltpu.HBM((128, HEADS * WIDTH), F32),
            pltpu.HBM((HEADS, PACK, WIDTH), F32),
            jax.ShapeDtypeStruct((HEADS, 8, WIDTH), F32),
            jax.ShapeDtypeStruct((HEADS, 4, WIDTH), F32),
        ],
        scratch_shapes=[
            pltpu.VMEM((2, HEADS, ROWS, WIDTH), F32),
            pltpu.VMEM((2, HEADS, 128, WIDTH), F32),
            pltpu.VMEM((2, HEADS, 64, WIDTH), F32),
            pltpu.VMEM((2, 8, WIDTH), F32),
            pltpu.SemaphoreType.DMA((2, HEADS)),
            pltpu.SemaphoreType.DMA((2, HEADS)),
            pltpu.SemaphoreType.DMA((2, HEADS)),
        ],
        compiler_params=params(20),
        cost_estimate=pl.CostEstimate(flops=2 << 20, bytes_accessed=10 << 20, transcendentals=0),
    )(in_hbm(k), in_hbm(v))


def pool_q_body(q_hbm, pay_in, q3_hbm, pay_hbm, rows, three, four, sems, sems3, sems4):
    def cols(h):
        return slice(WIDTH * h, WIDTH * h + WIDTH)

    def fetch(h):
        return pltpu.make_async_copy(q_hbm.at[:, cols(h)], rows.at[h], sems.at[h])

    def send3(h):
        return pltpu.make_async_copy(three.at[h], q3_hbm.at[:, cols(h)], sems3.at[h])

    def send4(h):
        return pltpu.make_async_copy(four.at[h], pay_hbm.at[h, 0:64, :], sems4.at[h])

    for h in range(HEADS):
        fetch(h).start()
    for h in range(HEADS):
        fetch(h).wait()
        three[h] = (0.125 * SCALE) * pool_eight(rows.at[h])
        send3(h).start()
        four[h] = pool_pairs(three.at[h], 64)
        send4(h).start()
    for h in range(HEADS):
        send3(h).wait()
        send4(h).wait()


def pool_q_call(q, pay):
    anywhere = pl.BlockSpec(memory_space=pl.ANY)
    return pl.pallas_call(
        pool_q_body,
        name="pool_queries",
        in_specs=[anywhere] * 2,
        out_specs=[anywhere] * 2,
        out_shape=[pltpu.HBM((128, HEADS * WIDTH), F32), pltpu.HBM((HEADS, PACK, WIDTH), F32)],
        input_output_aliases={1: 1},
        scratch_shapes=[
            pltpu.VMEM((HEADS, ROWS, WIDTH), F32),
            pltpu.VMEM((HEADS, 128, WIDTH), F32),
            pltpu.VMEM((HEADS, 64, WIDTH), F32),
            pltpu.SemaphoreType.DMA((HEADS,)),
            pltpu.SemaphoreType.DMA((HEADS,)),
            pltpu.SemaphoreType.DMA((HEADS,)),
        ],
        compiler_params=params(),
        cost_estimate=pl.CostEstimate(flops=2 << 30, bytes_accessed=5 << 20, transcendentals=0),
    )(in_hbm(q), in_hbm(pay))


def pack_body(pay_hbm, r8_ref, r9a_ref, r9b_ref, out_hbm, rows, sem):
    rows[:, 0:8, :] = r8_ref[...]
    rows[:, 8:12, :] = r9a_ref[...]
    rows[:, 12:16, :] = r9b_ref[...]
    copy = pltpu.make_async_copy(rows, out_hbm.at[:, 192:208, :], sem)
    copy.start()
    copy.wait()


def pack_call(pay, r8, r9a, r9b):
    vmem = pl.BlockSpec(memory_space=pltpu.VMEM)
    anywhere = pl.BlockSpec(memory_space=pl.ANY)
    return pl.pallas_call(
        pack_body,
        name="pack_rows",
        in_specs=[anywhere, vmem, vmem, vmem],
        out_specs=anywhere,
        out_shape=pltpu.HBM((HEADS, PACK, WIDTH), F32),
        input_output_aliases={0: 0},
        scratch_shapes=[pltpu.VMEM((HEADS, 16, WIDTH), F32), pltpu.SemaphoreType.DMA],
        compiler_params=params(4),
        cost_estimate=pl.CostEstimate(flops=0, bytes_accessed=1 << 17, transcendentals=0),
    )(in_hbm(pay), r8, r9a, r9b)


def local_body(count, q_ref, k_ref, v_ref, o_ref, lse_ref, columns):
    head = pl.program_id(0)

    def load(ref):
        return [ref[pl.ds(k, 128, stride=8), :] for k in range(8)]

    def pool(parts):
        return [0.5 * (parts[2 * i] + parts[2 * i + 1]) for i in range(len(parts) // 2)]

    def rows(parts, begin, count):
        return jnp.concatenate([x[begin : begin + count] for x in parts], axis=0)

    q0 = [x * SCALE for x in load(q_ref)]
    k0, v0 = load(k_ref), load(v_ref)
    q1, k1, v1 = pool(q0), pool(k0), pool(v0)
    q2, k2, v2 = pool(q1), pool(k1), pool(v1)
    tasks = []
    for b in range(2):
        c = 64 * (b ^ 1)
        tasks.append((rows(q2, 64 * b, 64), rows(k2, c, 64), rows(v2, c, 64), 2))
    for p in range(4):
        c = 32 * (p ^ 1)
        tasks.append((rows(q1, 32 * p, 32), rows(k1, c, 32), rows(v1, c, 32), 1))
    for p in range(4):
        c = 32 * p
        tasks.append((rows(q0, c, 32), rows(k0, c, 32), rows(v0, c, 32), 0))
    done = attend_all(tasks)
    at2, at1, at0 = done[:2], done[2:6], done[6:]

    lane = lax.broadcasted_iota(jnp.int32, (128, WIDTH), 1)
    lses = [[None] * 4 for _ in range(8)]
    for p in range(4):
        off = 32 * (p % 2)
        for j in range(4):
            i = j // 2
            one = tuple(x[32 * j : 32 * j + 32] for x in at1[p])
            two = tuple(x[64 * i + off : 64 * i + off + 32] for x in at2[p // 2])
            coarse = merge(one, two)
            for k in (2 * j, 2 * j + 1):
                m, s, n = merge(tuple(x[32 * k : 32 * k + 32] for x in at0[p]), coarse)
                o_ref[128 * k + 32 * p : 128 * k + 32 * p + 32, :] = n / s
                lses[k][p] = m + jnp.log2(s)
    for k in range(8):
        old = columns[128 * k : 128 * k + 128, :]
        columns[128 * k : 128 * k + 128, :] = jnp.where(lane == head, jnp.concatenate(lses[k], axis=0), old)

    @pl.when(head == count - 1)
    def _():
        for k in range(8):
            lse_ref[:, 128 * k : 128 * k + 128] = jnp.transpose(columns[128 * k : 128 * k + 128, :])[0:8]


def local_call(q, k, v, first, count, weight):
    block = pl.BlockSpec((ROWS, WIDTH), lambda h: (0, h + first))
    return pl.pallas_call(
        functools.partial(local_body, count),
        name="local_levels",
        grid=(count,),
        in_specs=[block] * 3,
        out_specs=[pl.BlockSpec((ROWS, WIDTH), lambda h: (0, h)), pl.BlockSpec((HEADS, ROWS), lambda h: (0, 0))],
        out_shape=[
            pltpu.HBM((ROWS, count * WIDTH), F32),
            pltpu.HBM((HEADS, ROWS), F32),
        ],
        scratch_shapes=[pltpu.VMEM((ROWS, WIDTH), F32)],
        compiler_params=params(16),
        cost_estimate=pl.CostEstimate(
            flops=count * weight << 20, bytes_accessed=count * weight << 11, transcendentals=count * weight << 9
        ),
    )(in_hbm(q), in_hbm(k), in_hbm(v))


def rise_body(got_ref, six_ref, seven_ref, scratch):
    for i in range(2):
        for s in range(8):
            scratch[i, 64 * s : 64 * s + 64, :] = got_ref[s, 64 * (i + 1) : 64 * (i + 2), :]
            scratch[i, 640 + 4 * s : 644 + 4 * s, :] = got_ref[s, 192 + 4 * i : 196 + 4 * i, :]
            for j in range(2):
                begin = 200 + 4 * j + 2 * i
                place = 672 + 16 * j + 2 * s
                scratch[i, place : place + 2, :] = got_ref[s, begin : begin + 2, :]
        x6 = scratch[i, pl.ds(0, 128, stride=4), :]
        for k in range(1, 4):
            x6 = x6 + scratch[i, pl.ds(k, 128, stride=4), :]
        x6 = 0.25 * x6
        scratch[i, 512:640, :] = x6
        six_ref[i, 0:128, :] = x6
        seven_ref[i, 0:64, :] = 0.5 * (
            scratch[i, pl.ds(512, 64, stride=2), :] + scratch[i, pl.ds(513, 64, stride=2), :]
        )
        six_ref[i, 128:192, :] = scratch[i, 640:704, :]
        seven_ref[i, 64:128, :] = scratch[i, 640:704, :]


def rise_call(got):
    return pl.pallas_call(
        rise_body,
        name="rise_rows",
        out_shape=[jax.ShapeDtypeStruct((2, n, WIDTH), F32) for n in (192, 128)],
        scratch_shapes=[pltpu.VMEM((2, 704, WIDTH), F32)],
        compiler_params=params(),
        cost_estimate=pl.CostEstimate(flops=1 << 18, bytes_accessed=1 << 19, transcendentals=0),
    )(got)


def middle_body(got_ref, o_ref, lse_ref, q_ref, scratch, es):
    for i in range(3):
        for s in range(8):
            scratch[i, 64 * s : 64 * s + 64, :] = got_ref[s, 64 * i : 64 * i + 64, :]
        base, count = 0, 256
        while count >= (16 if i == 0 else 256):
            x = pool_pairs(scratch.at[i, base : base + 2 * count], count)
            base = base + 2 * count
            scratch[i, base : base + count, :] = x
            count = count // 2
    q_ref[...] = scratch[0, 768:1008, :]
    tasks = []
    for level, base, blocks in ((4, 0, 4), (5, 512, 2)):
        for g in range(blocks):
            mine = slice(base + 128 * g, base + 128 * g + 128)
            other = slice(base + 128 * (g ^ 1), base + 128 * (g ^ 1) + 128)
            tasks.append((scratch[0, mine, :], scratch[1, other, :], scratch[2, other, :], level))
    done = attend_all(tasks)
    four, five = (tuple(jnp.concatenate(x, axis=0) for x in zip(*few)) for few in (done[0:4], done[4:6]))
    for i, x in enumerate(five):
        x = jnp.broadcast_to(x, (256, WIDTH))
        for c in range(2):
            es[i, pl.ds(c, 256, stride=2), :] = x
    m, s, n = merge(four, (es[0], es[1], es[2]))
    o_ref[...] = n / s
    lse_ref[...] = m + jnp.log2(s)


def middle_call(got):
    return pl.pallas_call(
        middle_body,
        name="middle_levels",
        out_shape=[jax.ShapeDtypeStruct((n, WIDTH), F32) for n in (512, 512, 240)],
        scratch_shapes=[pltpu.VMEM((3, 1024, WIDTH), F32), pltpu.VMEM((3, 512, WIDTH), F32)],
        compiler_params=params(),
        cost_estimate=pl.CostEstimate(flops=1 << 20, bytes_accessed=1 << 16, transcendentals=1 << 10),
    )(got)


def far_body(o_ref, lse_ref, q_ref, here_ref, six_ref, core_ref, seven_ref, out_ref, es):
    def sibling(i, level):
        if level == 6:
            return six_ref[i, 0:128, :]
        if level == 7:
            return jnp.concatenate([core_ref[i, 0:64, :], seven_ref[i, 0:64, :]], axis=0)
        low = 64 + 32 * (level - 8)
        return jnp.concatenate(
            [
                here_ref[i, 64 + low : 96 + low, :],
                core_ref[i, low : low + 32, :],
                six_ref[i, 64 + low : 96 + low, :],
                seven_ref[i, low : low + 32, :],
            ],
            axis=0,
        )

    tasks = []
    base, count = 0, 128
    for level in range(6, 10):
        tasks.append((q_ref[base : base + count, :], sibling(0, level), sibling(1, level), level))
        base, count = base + count, count // 2
    levels = attend_all(tasks)

    def spread(i, base, x, times):
        n = x.shape[0]
        x = jnp.broadcast_to(x, (n, WIDTH))
        for c in range(times):
            es[i, pl.ds(base + c, n, stride=times), :] = x
        return es[i, base : base + times * n, :]

    running = levels[-1]
    base = 0
    for finer in reversed(levels[:-1]):
        n = running[0].shape[0]
        running = merge(finer, tuple(spread(i, base, x, 2) for i, x in enumerate(running)))
        base = base + 2 * n
    m, s, n = running
    high_o, high_lse = spread(0, 256, n / s, 4), spread(1, 256, m + jnp.log2(s), 4)
    low_o, low_lse = o_ref[...], lse_ref[...]
    top = jnp.maximum(low_lse, high_lse)
    lse = top + jnp.log2(jnp.exp2(low_lse - top) + jnp.exp2(high_lse - top))
    o = high_o + (low_o - high_o) * share(low_lse, high_lse)
    for g in range(4):
        row = jnp.transpose(lse[128 * g : 128 * g + 128])[0:8]
        for d in range(2):
            out_ref[2 * g + d, 0:64, :] = o[128 * g + 64 * d : 128 * g + 64 * d + 64]
            out_ref[2 * g + d, 64:72, :] = row if d == 0 else pltpu.roll(row, 64, 1)


def far_call(middle, here, six, core, seven):
    return pl.pallas_call(
        far_body,
        name="far_levels",
        out_shape=pltpu.HBM((HEADS, BACK, WIDTH), F32),
        scratch_shapes=[pltpu.VMEM((3, 768, WIDTH), F32)],
        compiler_params=params(),
        cost_estimate=pl.CostEstimate(flops=100 << 20, bytes_accessed=1 << 20, transcendentals=1 << 17),
    )(*middle, here, six, core, seven)


def near_body(q3_ref, k3_ref, v3_ref, o_ref, lse_ref):
    lane = lax.broadcasted_iota(jnp.int32, (128, WIDTH), 1)
    packed = jnp.zeros((128, WIDTH), F32)
    cols = [slice(WIDTH * h, WIDTH * h + WIDTH) for h in range(HEADS)]
    done = attend_all([(q3_ref[:, c], k3_ref[:, c], v3_ref[:, c], 3) for c in cols])
    for h, (m, s, n) in enumerate(done):
        o_ref[:, cols[h]] = n / s
        packed = jnp.where(lane == h, m + jnp.log2(s), packed)
    lse_ref[...] = packed


def near_call(q3, k3, v3):
    return pl.pallas_call(
        near_body,
        name="near_level",
        out_shape=[pltpu.HBM((128, HEADS * WIDTH), F32), pltpu.HBM((128, WIDTH), F32)],
        compiler_params=params(),
        cost_estimate=pl.CostEstimate(flops=200 << 20, bytes_accessed=2 << 20, transcendentals=1 << 17),
    )(in_hbm(q3), k3, v3)


def join_body(*refs):
    n = len(CALLS)
    own_hbm, own_lse_hbm = refs[:n], refs[n : 2 * n]
    o3_hbm, lse3_hbm, far_ref, out_hbm = refs[2 * n : 2 * n + 4]
    own, own_lse, shares, o3, lse3, wide, stage, own_sems, sems, out_sems = refs[2 * n + 4 :]
    place = [(call, i) for call, count in enumerate(CALLS) for i in range(count)]

    def cols(h):
        return slice(WIDTH * h, WIDTH * h + WIDTH)

    def fetch(h):
        call, i = place[h]
        return pltpu.make_async_copy(own_hbm[call].at[:, cols(i)], own.at[h], own_sems.at[h])

    def send(h):
        return pltpu.make_async_copy(stage.at[h % 4], out_hbm.at[:, cols(h)], out_sems.at[h % 4])

    others = [pltpu.make_async_copy(lse3_hbm, lse3, sems.at[0]), pltpu.make_async_copy(o3_hbm, o3, sems.at[1])]
    others += [pltpu.make_async_copy(own_lse_hbm[call], own_lse.at[call], sems.at[call + 2]) for call in range(n)]
    for copy in others:
        copy.start()
    for h in range(HEADS):
        fetch(h).start()

    for h in range(HEADS):
        wide[1, h : h + 1, :] = far_ref[h, 64:65, :]
    far_lse = jnp.transpose(wide[1])[0:64]
    for c in range(2):
        wide[0, pl.ds(c, 64, stride=2), :] = far_lse
    far_lse = wide[0]
    for copy in others:
        copy.wait()
    near_lse = lse3[...]
    top = jnp.maximum(far_lse, near_lse)
    rest_lse = top + jnp.log2(jnp.exp2(far_lse - top) + jnp.exp2(near_lse - top))
    near_share = share(near_lse, far_lse)
    for h in range(HEADS):
        call, i = place[h]
        own_lse[n, h : h + 1, :] = own_lse[call, i : i + 1, :]
    for k in range(8):
        part = slice(128 * k, 128 * k + 128)
        lse = jnp.concatenate([own_lse[n, :, part], jnp.zeros((120, WIDTH), F32)], axis=0)
        shares[part, :] = share(jnp.transpose(lse), rest_lse)

    for h in range(HEADS):
        for c in range(2):
            wide[2 + h % 2, pl.ds(c, 64, stride=2), :] = far_ref[h, 0:64, :]
        far = wide[2 + h % 2]
        rest = far + (o3[:, cols(h)] - far) * jnp.broadcast_to(near_share[:, h : h + 1], (128, WIDTH))
        fetch(h).wait()
        if h >= 4:
            send(h - 4).wait()
        for k in range(8):
            part = slice(128 * k, 128 * k + 128)
            weight = jnp.broadcast_to(shares[part, h : h + 1], (128, WIDTH))
            stage[h % 4, pl.ds(k, 128, stride=8), :] = rest + (own[h, part, :] - rest) * weight
        send(h).start()
    for h in range(HEADS - 4, HEADS):
        send(h).wait()


def join_call(own, o3, lse3, far):
    n = len(CALLS)
    anywhere = pl.BlockSpec(memory_space=pl.ANY)
    return pl.pallas_call(
        join_body,
        name="join_levels",
        in_specs=[anywhere] * (2 * n + 2) + [pl.BlockSpec(memory_space=pltpu.VMEM)],
        out_specs=anywhere,
        out_shape=pltpu.HBM((ROWS, HEADS * WIDTH), F32),
        scratch_shapes=[
            pltpu.VMEM((HEADS, ROWS, WIDTH), F32),
            pltpu.VMEM((n + 1, HEADS, ROWS), F32),
            pltpu.VMEM((ROWS, WIDTH), F32),
            pltpu.VMEM((128, HEADS * WIDTH), F32),
            pltpu.VMEM((128, WIDTH), F32),
            pltpu.VMEM((4, 128, WIDTH), F32),
            pltpu.VMEM((4, ROWS, WIDTH), F32),
            pltpu.SemaphoreType.DMA((HEADS,)),
            pltpu.SemaphoreType.DMA((n + 2,)),
            pltpu.SemaphoreType.DMA((4,)),
        ],
        compiler_params=params(20),
        cost_estimate=pl.CostEstimate(flops=16 << 20, bytes_accessed=9 << 20, transcendentals=1 << 20),
    )(*[in_hbm(o) for o, _ in own], *[in_hbm(lse) for _, lse in own], in_hbm(o3), in_hbm(lse3), far)


def hop(x, axis, flip):
    return lax.ppermute(x, axis, [(i, i ^ flip) for i in range(lax.axis_size(axis))])


def transpose_heads(x):
    return lax.all_to_all(x, "node", 0, 0, axis_index_groups=GROUPS, tiled=True)


def on_device(queries, keys, values):
    k3, v3, pay, x8, x9 = pool_kv_call(keys, values)
    first = [sum(CALLS[:i]) for i in range(len(CALLS))]
    local = []

    def local_part(i, *after, weight=1024):
        q, k, v = lax.optimization_barrier((queries, keys, values) + after)[:3]
        return local_call(q, k, v, first[i], CALLS[i], weight)

    r8, r9a, r9b = hop(x8, "seq", 2), hop(x9, "seq", 4), hop(x9, "seq", 6)
    q3, pay = pool_q_call(queries, pay)
    pay = pack_call(pay, r8, r9a, r9b)
    got = transpose_heads(pay)
    part = local_part(0, pay, weight=4096)
    got, part = lax.optimization_barrier((got, part))
    local.append(part)
    _, k3, v3 = lax.optimization_barrier((part, k3, v3))
    sib_k3, sib_v3 = hop(k3, "node", 1), hop(v3, "node", 1)

    here6, here7 = rise_call(got)
    six = hop(here6, "node", 12)
    core = hop(here7, "seq", 1)
    seven = hop(core, "node", 12)
    middle = middle_call(lax.optimization_barrier((got, core))[0])
    part = local_part(1, core, weight=1)
    six, seven, part, middle = lax.optimization_barrier((six, seven, part, middle))
    local.append(part)

    far = far_call(middle, here6, six, core, seven)
    back = transpose_heads(far)
    local.append(local_part(2, far, sib_k3))
    q3 = lax.optimization_barrier((q3, local[-1]))[0]
    o3, lse3 = near_call(q3, sib_k3, sib_v3)
    return join_call(local, o3, lse3, back)


def solution(mesh):
    spec = P(("seq", "node"), None)
    return jax.shard_map(on_device, mesh=mesh, in_specs=(spec, spec, spec), out_specs=spec, check_vma=False)
```

```python
import functools
import math

import jax
import jax.numpy as jnp
from jax import lax
from jax.experimental import pallas as pl
from jax.experimental.pallas import tpu as pltpu
from jax.sharding import PartitionSpec as P

HEADS = 8
PACK = 208
BACK = 72
CALLS = (5, 2, 1)
WIDTH = 128
ROWS = 1024
F32 = jnp.float32
BF16 = jnp.bfloat16
SCALE = WIDTH ** (-0.5) / math.log(2.0)
MIB = 1024 * 1024

GROUPS = [list(range(8)), [12, 13, 14, 15, 8, 9, 10, 11]]


def params(mib=12):
    return pltpu.CompilerParams(vmem_limit_bytes=mib * MIB)


def in_hbm(x):
    return pltpu.with_memory_space_constraint(x, pltpu.HBM)


def split(x):
    hi = x.astype(BF16)
    lo = (x - hi.astype(F32)).astype(BF16)
    return hi, lo


def dot_nt(a, b):
    return lax.dot_general(a, b, (((1,), (1,)), ((), ())), preferred_element_type=F32)


def dot_nn(a, b):
    return lax.dot_general(a, b, (((1,), (0,)), ((), ())), preferred_element_type=F32)


def key_side(k):
    hi, lo = split(k)
    return jnp.concatenate([hi, hi], axis=1), jnp.concatenate([lo, jnp.zeros_like(lo)], axis=1)


def scores(q, sides):
    hi, lo = split(q)
    both = jnp.concatenate([hi, lo], axis=1)
    first, second = sides
    n = first.shape[0]
    if n == 128:
        s = dot_nt(both, jnp.concatenate([first, second], axis=0))
        return s[:, :n] + s[:, n:]
    return dot_nt(both, first) + dot_nt(both, second)


def weigh(p, side):
    hi, lo = side
    p_hi, p_lo = split(p)
    if hi.shape[0] == 128:
        left = jnp.concatenate([p_hi, p_lo], axis=1)
        right = jnp.concatenate(
            [jnp.concatenate([hi, lo], axis=1), jnp.concatenate([hi, jnp.zeros_like(lo)], axis=1)], axis=0
        )
        r = dot_nn(left, right)
        return r[:, :WIDTH] + r[:, WIDTH:]
    r = dot_nn(p_hi, jnp.concatenate([hi, lo], axis=1))
    return r[:, :WIDTH] + r[:, WIDTH:] + dot_nn(p_lo, hi)


def attend_all(tasks):
    grids = [scores(q, key_side(k)) for q, k, _, _ in tasks]
    peaks = [jnp.max(s, axis=1, keepdims=True) for s in grids]
    weights = [jnp.exp2(s - peak) for s, peak in zip(grids, peaks)]
    totals = [jnp.sum(p, axis=1, keepdims=True) for p in weights]
    numerators = [weigh(p, split(task[2])) for p, task in zip(weights, tasks)]
    return [(peak + float(task[3]), t, n) for peak, t, n, task in zip(peaks, totals, numerators, tasks)]


def merge(a, b):
    ma, sa, na = a
    mb, sb, nb = b
    m = jnp.maximum(ma, mb)
    fa, fb = jnp.exp2(ma - m), jnp.exp2(mb - m)
    return m, sa * fa + sb * fb, na * fa + nb * fb


def share(a, b):
    return 1.0 / (1.0 + jnp.exp2(b - a))


def pool_eight(ref):
    total = ref[pl.ds(0, 128, stride=8), :]
    for k in range(1, 8):
        total = total + ref[pl.ds(k, 128, stride=8), :]
    return total


def pool_pairs(ref, n):
    return 0.5 * (ref[pl.ds(0, n, stride=2), :] + ref[pl.ds(1, n, stride=2), :])


def pool_kv_body(k_hbm, v_hbm, k3_hbm, v3_hbm, pay_hbm, x8_ref, x9_ref, rows, three, four, more, sems, sems3, sems4):
    arrays, outs = (k_hbm, v_hbm), (k3_hbm, v3_hbm)

    def cols(h):
        return slice(WIDTH * h, WIDTH * h + WIDTH)

    def fetch(i, h):
        return pltpu.make_async_copy(arrays[i].at[:, cols(h)], rows.at[i, h], sems.at[i, h])

    def send3(i, h):
        return pltpu.make_async_copy(three.at[i, h], outs[i].at[:, cols(h)], sems3.at[i, h])

    def send4(i, h):
        return pltpu.make_async_copy(four.at[i, h], pay_hbm.at[h, 64 * i + 64 : 64 * i + 128, :], sems4.at[i, h])

    every = [(i, h) for h in range(HEADS) for i in range(2)]
    for i, h in every:
        fetch(i, h).start()
    for i, h in every:
        fetch(i, h).wait()
        three[i, h] = 0.125 * pool_eight(rows.at[i, h])
        send3(i, h).start()
        four[i, h] = pool_pairs(three.at[i, h], 64)
        send4(i, h).start()
        x7 = four[i, h, pl.ds(0, 8, stride=8), :]
        for k in range(1, 8):
            x7 = x7 + four[i, h, pl.ds(k, 8, stride=8), :]
        more[i] = 0.125 * x7
        x8 = pool_pairs(more.at[i], 4)
        x8_ref[h, 4 * i : 4 * i + 4, :] = x8
        x9_ref[h, 2 * i : 2 * i + 2, :] = jnp.concatenate(
            [0.5 * (x8[0:1] + x8[1:2]), 0.5 * (x8[2:3] + x8[3:4])], axis=0
        )
    for i, h in every:
        send3(i, h).wait()
        send4(i, h).wait()


def pool_kv_call(k, v):
    anywhere = pl.BlockSpec(memory_space=pl.ANY)
    vmem = pl.BlockSpec(memory_space=pltpu.VMEM)
    return pl.pallas_call(
        pool_kv_body,
        name="pool_keys",
        in_specs=[anywhere] * 2,
        out_specs=[anywhere] * 3 + [vmem] * 2,
        out_shape=[
            pltpu.HBM((128, HEADS * WIDTH), F32),
            pltpu.HBM((128, HEADS * WIDTH), F32),
            pltpu.HBM((HEADS, PACK, WIDTH), F32),
            jax.ShapeDtypeStruct((HEADS, 8, WIDTH), F32),
            jax.ShapeDtypeStruct((HEADS, 4, WIDTH), F32),
        ],
        scratch_shapes=[
            pltpu.VMEM((2, HEADS, ROWS, WIDTH), F32),
            pltpu.VMEM((2, HEADS, 128, WIDTH), F32),
            pltpu.VMEM((2, HEADS, 64, WIDTH), F32),
            pltpu.VMEM((2, 8, WIDTH), F32),
            pltpu.SemaphoreType.DMA((2, HEADS)),
            pltpu.SemaphoreType.DMA((2, HEADS)),
            pltpu.SemaphoreType.DMA((2, HEADS)),
        ],
        compiler_params=params(20),
        cost_estimate=pl.CostEstimate(flops=2 << 20, bytes_accessed=10 << 20, transcendentals=0),
    )(in_hbm(k), in_hbm(v))


def pool_q_body(q_hbm, pay_in, q3_hbm, pay_hbm, rows, three, four, sems, sems3, sems4):
    def cols(h):
        return slice(WIDTH * h, WIDTH * h + WIDTH)

    def fetch(h):
        return pltpu.make_async_copy(q_hbm.at[:, cols(h)], rows.at[h], sems.at[h])

    def send3(h):
        return pltpu.make_async_copy(three.at[h], q3_hbm.at[:, cols(h)], sems3.at[h])

    def send4(h):
        return pltpu.make_async_copy(four.at[h], pay_hbm.at[h, 0:64, :], sems4.at[h])

    for h in range(HEADS):
        fetch(h).start()
    for h in range(HEADS):
        fetch(h).wait()
        three[h] = (0.125 * SCALE) * pool_eight(rows.at[h])
        send3(h).start()
        four[h] = pool_pairs(three.at[h], 64)
        send4(h).start()
    for h in range(HEADS):
        send3(h).wait()
        send4(h).wait()


def pool_q_call(q, pay):
    anywhere = pl.BlockSpec(memory_space=pl.ANY)
    return pl.pallas_call(
        pool_q_body,
        name="pool_queries",
        in_specs=[anywhere] * 2,
        out_specs=[anywhere] * 2,
        out_shape=[pltpu.HBM((128, HEADS * WIDTH), F32), pltpu.HBM((HEADS, PACK, WIDTH), F32)],
        input_output_aliases={1: 1},
        scratch_shapes=[
            pltpu.VMEM((HEADS, ROWS, WIDTH), F32),
            pltpu.VMEM((HEADS, 128, WIDTH), F32),
            pltpu.VMEM((HEADS, 64, WIDTH), F32),
            pltpu.SemaphoreType.DMA((HEADS,)),
            pltpu.SemaphoreType.DMA((HEADS,)),
            pltpu.SemaphoreType.DMA((HEADS,)),
        ],
        compiler_params=params(),
        cost_estimate=pl.CostEstimate(flops=2 << 30, bytes_accessed=5 << 20, transcendentals=0),
    )(in_hbm(q), in_hbm(pay))


def pack_body(pay_hbm, r8_ref, r9a_ref, r9b_ref, out_hbm, rows, sem):
    rows[:, 0:8, :] = r8_ref[...]
    rows[:, 8:12, :] = r9a_ref[...]
    rows[:, 12:16, :] = r9b_ref[...]
    copy = pltpu.make_async_copy(rows, out_hbm.at[:, 192:208, :], sem)
    copy.start()
    copy.wait()


def pack_call(pay, r8, r9a, r9b):
    vmem = pl.BlockSpec(memory_space=pltpu.VMEM)
    anywhere = pl.BlockSpec(memory_space=pl.ANY)
    return pl.pallas_call(
        pack_body,
        name="pack_rows",
        in_specs=[anywhere, vmem, vmem, vmem],
        out_specs=anywhere,
        out_shape=pltpu.HBM((HEADS, PACK, WIDTH), F32),
        input_output_aliases={0: 0},
        scratch_shapes=[pltpu.VMEM((HEADS, 16, WIDTH), F32), pltpu.SemaphoreType.DMA],
        compiler_params=params(4),
        cost_estimate=pl.CostEstimate(flops=0, bytes_accessed=1 << 17, transcendentals=0),
    )(in_hbm(pay), r8, r9a, r9b)


def local_body(count, q_ref, k_ref, v_ref, o_ref, lse_ref, columns):
    head = pl.program_id(0)

    def load(ref):
        return [ref[pl.ds(k, 128, stride=8), :] for k in range(8)]

    def pool(parts):
        return [0.5 * (parts[2 * i] + parts[2 * i + 1]) for i in range(len(parts) // 2)]

    def rows(parts, begin, count):
        return jnp.concatenate([x[begin : begin + count] for x in parts], axis=0)

    q0 = [x * SCALE for x in load(q_ref)]
    k0, v0 = load(k_ref), load(v_ref)
    q1, k1, v1 = pool(q0), pool(k0), pool(v0)
    q2, k2, v2 = pool(q1), pool(k1), pool(v1)
    tasks = []
    for b in range(2):
        c = 64 * (b ^ 1)
        tasks.append((rows(q2, 64 * b, 64), rows(k2, c, 64), rows(v2, c, 64), 2))
    for p in range(4):
        c = 32 * (p ^ 1)
        tasks.append((rows(q1, 32 * p, 32), rows(k1, c, 32), rows(v1, c, 32), 1))
    for p in range(4):
        c = 32 * p
        tasks.append((rows(q0, c, 32), rows(k0, c, 32), rows(v0, c, 32), 0))
    done = attend_all(tasks)
    at2, at1, at0 = done[:2], done[2:6], done[6:]

    lane = lax.broadcasted_iota(jnp.int32, (128, WIDTH), 1)
    lses = [[None] * 4 for _ in range(8)]
    for p in range(4):
        off = 32 * (p % 2)
        for j in range(4):
            i = j // 2
            one = tuple(x[32 * j : 32 * j + 32] for x in at1[p])
            two = tuple(x[64 * i + off : 64 * i + off + 32] for x in at2[p // 2])
            coarse = merge(one, two)
            for k in (2 * j, 2 * j + 1):
                m, s, n = merge(tuple(x[32 * k : 32 * k + 32] for x in at0[p]), coarse)
                o_ref[128 * k + 32 * p : 128 * k + 32 * p + 32, :] = n / s
                lses[k][p] = m + jnp.log2(s)
    for k in range(8):
        old = columns[128 * k : 128 * k + 128, :]
        columns[128 * k : 128 * k + 128, :] = jnp.where(lane == head, jnp.concatenate(lses[k], axis=0), old)

    @pl.when(head == count - 1)
    def _():
        for k in range(8):
            lse_ref[:, 128 * k : 128 * k + 128] = jnp.transpose(columns[128 * k : 128 * k + 128, :])[0:8]


def local_call(q, k, v, first, count, weight):
    block = pl.BlockSpec((ROWS, WIDTH), lambda h: (0, h + first))
    return pl.pallas_call(
        functools.partial(local_body, count),
        name="local_levels",
        grid=(count,),
        in_specs=[block] * 3,
        out_specs=[pl.BlockSpec((ROWS, WIDTH), lambda h: (0, h)), pl.BlockSpec((HEADS, ROWS), lambda h: (0, 0))],
        out_shape=[
            pltpu.HBM((ROWS, count * WIDTH), F32),
            pltpu.HBM((HEADS, ROWS), F32),
        ],
        scratch_shapes=[pltpu.VMEM((ROWS, WIDTH), F32)],
        compiler_params=params(16),
        cost_estimate=pl.CostEstimate(
            flops=count * weight << 20, bytes_accessed=count * weight << 11, transcendentals=count * weight << 9
        ),
    )(in_hbm(q), in_hbm(k), in_hbm(v))


def rise_body(got_ref, six_ref, seven_ref, scratch):
    for i in range(2):
        for s in range(8):
            scratch[i, 64 * s : 64 * s + 64, :] = got_ref[s, 64 * (i + 1) : 64 * (i + 2), :]
            scratch[i, 640 + 4 * s : 644 + 4 * s, :] = got_ref[s, 192 + 4 * i : 196 + 4 * i, :]
            for j in range(2):
                begin = 200 + 4 * j + 2 * i
                place = 672 + 16 * j + 2 * s
                scratch[i, place : place + 2, :] = got_ref[s, begin : begin + 2, :]
        x6 = scratch[i, pl.ds(0, 128, stride=4), :]
        for k in range(1, 4):
            x6 = x6 + scratch[i, pl.ds(k, 128, stride=4), :]
        x6 = 0.25 * x6
        scratch[i, 512:640, :] = x6
        six_ref[i, 0:128, :] = x6
        seven_ref[i, 0:64, :] = 0.5 * (
            scratch[i, pl.ds(512, 64, stride=2), :] + scratch[i, pl.ds(513, 64, stride=2), :]
        )
        six_ref[i, 128:192, :] = scratch[i, 640:704, :]
        seven_ref[i, 64:128, :] = scratch[i, 640:704, :]


def rise_call(got):
    return pl.pallas_call(
        rise_body,
        name="rise_rows",
        out_shape=[jax.ShapeDtypeStruct((2, n, WIDTH), F32) for n in (192, 128)],
        scratch_shapes=[pltpu.VMEM((2, 704, WIDTH), F32)],
        compiler_params=params(),
        cost_estimate=pl.CostEstimate(flops=1 << 18, bytes_accessed=1 << 19, transcendentals=0),
    )(got)


def middle_body(got_ref, o_ref, lse_ref, q_ref, scratch, es):
    for i in range(3):
        for s in range(8):
            scratch[i, 64 * s : 64 * s + 64, :] = got_ref[s, 64 * i : 64 * i + 64, :]
        base, count = 0, 256
        while count >= (16 if i == 0 else 256):
            x = pool_pairs(scratch.at[i, base : base + 2 * count], count)
            base = base + 2 * count
            scratch[i, base : base + count, :] = x
            count = count // 2
    q_ref[...] = scratch[0, 768:1008, :]
    tasks = []
    for level, base, blocks in ((4, 0, 4), (5, 512, 2)):
        for g in range(blocks):
            mine = slice(base + 128 * g, base + 128 * g + 128)
            other = slice(base + 128 * (g ^ 1), base + 128 * (g ^ 1) + 128)
            tasks.append((scratch[0, mine, :], scratch[1, other, :], scratch[2, other, :], level))
    done = attend_all(tasks)
    four, five = (tuple(jnp.concatenate(x, axis=0) for x in zip(*few)) for few in (done[0:4], done[4:6]))
    for i, x in enumerate(five):
        x = jnp.broadcast_to(x, (256, WIDTH))
        for c in range(2):
            es[i, pl.ds(c, 256, stride=2), :] = x
    m, s, n = merge(four, (es[0], es[1], es[2]))
    o_ref[...] = n / s
    lse_ref[...] = m + jnp.log2(s)


def middle_call(got):
    return pl.pallas_call(
        middle_body,
        name="middle_levels",
        out_shape=[jax.ShapeDtypeStruct((n, WIDTH), F32) for n in (512, 512, 240)],
        scratch_shapes=[pltpu.VMEM((3, 1024, WIDTH), F32), pltpu.VMEM((3, 512, WIDTH), F32)],
        compiler_params=params(),
        cost_estimate=pl.CostEstimate(flops=1 << 20, bytes_accessed=1 << 16, transcendentals=1 << 10),
    )(got)


def far_body(o_ref, lse_ref, q_ref, here_ref, six_ref, core_ref, seven_ref, out_ref, es):
    def sibling(i, level):
        if level == 6:
            return six_ref[i, 0:128, :]
        if level == 7:
            return jnp.concatenate([core_ref[i, 0:64, :], seven_ref[i, 0:64, :]], axis=0)
        low = 64 + 32 * (level - 8)
        return jnp.concatenate(
            [
                here_ref[i, 64 + low : 96 + low, :],
                core_ref[i, low : low + 32, :],
                six_ref[i, 64 + low : 96 + low, :],
                seven_ref[i, low : low + 32, :],
            ],
            axis=0,
        )

    tasks = []
    base, count = 0, 128
    for level in range(6, 10):
        tasks.append((q_ref[base : base + count, :], sibling(0, level), sibling(1, level), level))
        base, count = base + count, count // 2
    levels = attend_all(tasks)

    def spread(i, base, x, times):
        n = x.shape[0]
        x = jnp.broadcast_to(x, (n, WIDTH))
        for c in range(times):
            es[i, pl.ds(base + c, n, stride=times), :] = x
        return es[i, base : base + times * n, :]

    running = levels[-1]
    base = 0
    for finer in reversed(levels[:-1]):
        n = running[0].shape[0]
        running = merge(finer, tuple(spread(i, base, x, 2) for i, x in enumerate(running)))
        base = base + 2 * n
    m, s, n = running
    high_o, high_lse = spread(0, 256, n / s, 4), spread(1, 256, m + jnp.log2(s), 4)
    low_o, low_lse = o_ref[...], lse_ref[...]
    top = jnp.maximum(low_lse, high_lse)
    lse = top + jnp.log2(jnp.exp2(low_lse - top) + jnp.exp2(high_lse - top))
    o = high_o + (low_o - high_o) * share(low_lse, high_lse)
    for g in range(4):
        row = jnp.transpose(lse[128 * g : 128 * g + 128])[0:8]
        for d in range(2):
            out_ref[2 * g + d, 0:64, :] = o[128 * g + 64 * d : 128 * g + 64 * d + 64]
            out_ref[2 * g + d, 64:72, :] = row if d == 0 else pltpu.roll(row, 64, 1)


def far_call(middle, here, six, core, seven):
    return pl.pallas_call(
        far_body,
        name="far_levels",
        out_shape=pltpu.HBM((HEADS, BACK, WIDTH), F32),
        scratch_shapes=[pltpu.VMEM((3, 768, WIDTH), F32)],
        compiler_params=params(),
        cost_estimate=pl.CostEstimate(flops=100 << 20, bytes_accessed=1 << 20, transcendentals=1 << 17),
    )(*middle, here, six, core, seven)


def near_body(q3_ref, k3_ref, v3_ref, o_ref, lse_ref):
    lane = lax.broadcasted_iota(jnp.int32, (128, WIDTH), 1)
    packed = jnp.zeros((128, WIDTH), F32)
    cols = [slice(WIDTH * h, WIDTH * h + WIDTH) for h in range(HEADS)]
    done = attend_all([(q3_ref[:, c], k3_ref[:, c], v3_ref[:, c], 3) for c in cols])
    for h, (m, s, n) in enumerate(done):
        o_ref[:, cols[h]] = n / s
        packed = jnp.where(lane == h, m + jnp.log2(s), packed)
    lse_ref[...] = packed


def near_call(q3, k3, v3):
    return pl.pallas_call(
        near_body,
        name="near_level",
        out_shape=[pltpu.HBM((128, HEADS * WIDTH), F32), pltpu.HBM((128, WIDTH), F32)],
        compiler_params=params(),
        cost_estimate=pl.CostEstimate(flops=200 << 20, bytes_accessed=2 << 20, transcendentals=1 << 17),
    )(in_hbm(q3), k3, v3)


def join_body(*refs):
    n = len(CALLS)
    own_hbm, own_lse_hbm = refs[:n], refs[n : 2 * n]
    o3_hbm, lse3_hbm, far_ref, out_hbm = refs[2 * n : 2 * n + 4]
    own, own_lse, shares, o3, lse3, wide, stage, own_sems, sems, out_sems = refs[2 * n + 4 :]
    place = [(call, i) for call, count in enumerate(CALLS) for i in range(count)]
    late = range(CALLS[0], HEADS)

    def cols(h):
        return slice(WIDTH * h, WIDTH * h + WIDTH)

    def fetch(h):
        call, i = place[h]
        j = h - CALLS[0]
        return pltpu.make_async_copy(own_hbm[call].at[:, cols(i)], own.at[j], own_sems.at[j])

    def results(h, part):
        if h in late:
            return own[h - CALLS[0], part, :]
        return own_hbm[0][part, cols(h)]

    def send(h):
        return pltpu.make_async_copy(stage.at[h % 4], out_hbm.at[:, cols(h)], out_sems.at[h % 4])

    others = [pltpu.make_async_copy(lse3_hbm, lse3, sems.at[0]), pltpu.make_async_copy(o3_hbm, o3, sems.at[1])]
    others += [pltpu.make_async_copy(own_lse_hbm[call], own_lse.at[call], sems.at[call + 2]) for call in range(n)]
    for copy in others:
        copy.start()
    for h in late:
        fetch(h).start()

    for h in range(HEADS):
        wide[1, h : h + 1, :] = far_ref[h, 64:65, :]
    far_lse = jnp.transpose(wide[1])[0:64]
    for c in range(2):
        wide[0, pl.ds(c, 64, stride=2), :] = far_lse
    far_lse = wide[0]
    for copy in others:
        copy.wait()
    near_lse = lse3[...]
    top = jnp.maximum(far_lse, near_lse)
    rest_lse = top + jnp.log2(jnp.exp2(far_lse - top) + jnp.exp2(near_lse - top))
    near_share = share(near_lse, far_lse)
    for h in range(HEADS):
        call, i = place[h]
        own_lse[n, h : h + 1, :] = own_lse[call, i : i + 1, :]
    for k in range(8):
        part = slice(128 * k, 128 * k + 128)
        lse = jnp.concatenate([own_lse[n, :, part], jnp.zeros((120, WIDTH), F32)], axis=0)
        shares[part, :] = share(jnp.transpose(lse), rest_lse)

    for h in range(HEADS):
        for c in range(2):
            wide[2 + h % 2, pl.ds(c, 64, stride=2), :] = far_ref[h, 0:64, :]
        far = wide[2 + h % 2]
        rest = far + (o3[:, cols(h)] - far) * jnp.broadcast_to(near_share[:, h : h + 1], (128, WIDTH))
        if h in late:
            fetch(h).wait()
        if h >= 4:
            send(h - 4).wait()
        for k in range(8):
            part = slice(128 * k, 128 * k + 128)
            weight = jnp.broadcast_to(shares[part, h : h + 1], (128, WIDTH))
            stage[h % 4, pl.ds(k, 128, stride=8), :] = rest + (results(h, part) - rest) * weight
        send(h).start()
    for h in range(HEADS - 4, HEADS):
        send(h).wait()


def join_call(own, o3, lse3, far):
    n = len(CALLS)
    vmem = pl.BlockSpec(memory_space=pltpu.VMEM)
    anywhere = pl.BlockSpec(memory_space=pl.ANY)
    return pl.pallas_call(
        join_body,
        name="join_levels",
        in_specs=[vmem] + [anywhere] * (2 * n + 1) + [vmem],
        out_specs=anywhere,
        out_shape=pltpu.HBM((ROWS, HEADS * WIDTH), F32),
        scratch_shapes=[
            pltpu.VMEM((HEADS - CALLS[0], ROWS, WIDTH), F32),
            pltpu.VMEM((n + 1, HEADS, ROWS), F32),
            pltpu.VMEM((ROWS, WIDTH), F32),
            pltpu.VMEM((128, HEADS * WIDTH), F32),
            pltpu.VMEM((128, WIDTH), F32),
            pltpu.VMEM((4, 128, WIDTH), F32),
            pltpu.VMEM((4, ROWS, WIDTH), F32),
            pltpu.SemaphoreType.DMA((HEADS - CALLS[0],)),
            pltpu.SemaphoreType.DMA((n + 2,)),
            pltpu.SemaphoreType.DMA((4,)),
        ],
        compiler_params=params(14),
        cost_estimate=pl.CostEstimate(flops=16 << 20, bytes_accessed=9 << 20, transcendentals=1 << 20),
    )(own[0][0], *[in_hbm(o) for o, _ in own[1:]], *[in_hbm(lse) for _, lse in own], in_hbm(o3), in_hbm(lse3), far)


def hop(x, axis, flip):
    return lax.ppermute(x, axis, [(i, i ^ flip) for i in range(lax.axis_size(axis))])


def transpose_heads(x):
    return lax.all_to_all(x, "node", 0, 0, axis_index_groups=GROUPS, tiled=True)


def on_device(queries, keys, values):
    k3, v3, pay, x8, x9 = pool_kv_call(keys, values)
    sib_k3 = hop(k3, "node", 1)
    first = [sum(CALLS[:i]) for i in range(len(CALLS))]
    local = []

    def local_part(i, *after, weight=1024):
        q, k, v = lax.optimization_barrier((queries, keys, values) + after)[:3]
        return local_call(q, k, v, first[i], CALLS[i], weight)

    r8, r9a, r9b = hop(x8, "seq", 2), hop(x9, "seq", 4), hop(x9, "seq", 6)
    q3, pay = pool_q_call(queries, pay)
    pay = pack_call(pay, r8, r9a, r9b)
    got = transpose_heads(pay)
    part = local_part(0, pay, weight=1)
    got, part = lax.optimization_barrier((got, part))
    local.append(part)
    v3 = lax.optimization_barrier((part, v3))[1]
    sib_v3 = hop(v3, "node", 1)

    here6, here7 = rise_call(got)
    six = hop(here6, "node", 12)
    core = hop(here7, "seq", 1)
    seven = hop(core, "node", 12)
    middle = middle_call(lax.optimization_barrier((got, core))[0])
    part = local_part(1, core, weight=1)
    six, seven, part, middle = lax.optimization_barrier((six, seven, part, middle))
    local.append(part)

    far = far_call(middle, here6, six, core, seven)
    back = transpose_heads(far)
    local.append(local_part(2, far, sib_k3))
    q3 = lax.optimization_barrier((q3, local[-1]))[0]
    o3, lse3 = near_call(q3, sib_k3, sib_v3)
    return join_call(local, o3, lse3, back)


def solution(mesh):
    spec = P(("seq", "node"), None)
    return jax.shard_map(on_device, mesh=mesh, in_specs=(spec, spec, spec), out_specs=spec, check_vma=False)
```

```python
import functools
import math

import jax
import jax.numpy as jnp
from jax import lax
from jax.experimental import pallas as pl
from jax.experimental.pallas import tpu as pltpu
from jax.sharding import PartitionSpec as P

HEADS = 8
PACK = 208
BACK = 72
CALLS = (5, 2, 1)
WIDTH = 128
ROWS = 1024
F32 = jnp.float32
BF16 = jnp.bfloat16
SCALE = WIDTH ** (-0.5) / math.log(2.0)
MIB = 1024 * 1024

GROUPS = [list(range(8)), [12, 13, 14, 15, 8, 9, 10, 11]]


def params(mib=12):
    return pltpu.CompilerParams(vmem_limit_bytes=mib * MIB)


def in_hbm(x):
    return pltpu.with_memory_space_constraint(x, pltpu.HBM)


def split(x):
    hi = x.astype(BF16)
    lo = (x - hi.astype(F32)).astype(BF16)
    return hi, lo


def dot_nt(a, b):
    return lax.dot_general(a, b, (((1,), (1,)), ((), ())), preferred_element_type=F32)


def dot_nn(a, b):
    return lax.dot_general(a, b, (((1,), (0,)), ((), ())), preferred_element_type=F32)


def key_side(k):
    hi, lo = split(k)
    return jnp.concatenate([hi, hi], axis=1), jnp.concatenate([lo, jnp.zeros_like(lo)], axis=1)


def scores(q, sides):
    hi, lo = split(q)
    both = jnp.concatenate([hi, lo], axis=1)
    first, second = sides
    n = first.shape[0]
    if n == 128:
        s = dot_nt(both, jnp.concatenate([first, second], axis=0))
        return s[:, :n] + s[:, n:]
    return dot_nt(both, first) + dot_nt(both, second)


def weigh(p, side):
    hi, lo = side
    p_hi, p_lo = split(p)
    if hi.shape[0] == 128:
        left = jnp.concatenate([p_hi, p_lo], axis=1)
        right = jnp.concatenate(
            [jnp.concatenate([hi, lo], axis=1), jnp.concatenate([hi, jnp.zeros_like(lo)], axis=1)], axis=0
        )
        r = dot_nn(left, right)
        return r[:, :WIDTH] + r[:, WIDTH:]
    r = dot_nn(p_hi, jnp.concatenate([hi, lo], axis=1))
    return r[:, :WIDTH] + r[:, WIDTH:] + dot_nn(p_lo, hi)


def attend_all(tasks):
    grids = [scores(q, key_side(k)) for q, k, _, _ in tasks]
    peaks = [jnp.max(s, axis=1, keepdims=True) for s in grids]
    weights = [jnp.exp2(s - peak) for s, peak in zip(grids, peaks)]
    totals = [jnp.sum(p, axis=1, keepdims=True) for p in weights]
    numerators = [weigh(p, split(task[2])) for p, task in zip(weights, tasks)]
    return [(peak + float(task[3]), t, n) for peak, t, n, task in zip(peaks, totals, numerators, tasks)]


def merge(a, b):
    ma, sa, na = a
    mb, sb, nb = b
    m = jnp.maximum(ma, mb)
    fa, fb = jnp.exp2(ma - m), jnp.exp2(mb - m)
    return m, sa * fa + sb * fb, na * fa + nb * fb


def share(a, b):
    return 1.0 / (1.0 + jnp.exp2(b - a))


def pool_eight(ref):
    total = ref[pl.ds(0, 128, stride=8), :]
    for k in range(1, 8):
        total = total + ref[pl.ds(k, 128, stride=8), :]
    return total


def pool_pairs(ref, n):
    return 0.5 * (ref[pl.ds(0, n, stride=2), :] + ref[pl.ds(1, n, stride=2), :])


def pool_kv_body(k_hbm, v_hbm, k3_hbm, v3_hbm, pay_hbm, x8_ref, x9_ref, rows, three, four, more, sems, sems3, sems4):
    arrays, outs = (k_hbm, v_hbm), (k3_hbm, v3_hbm)

    def cols(h):
        return slice(WIDTH * h, WIDTH * h + WIDTH)

    def fetch(i, h):
        return pltpu.make_async_copy(arrays[i].at[:, cols(h)], rows.at[i, h], sems.at[i, h])

    def send3(i, h):
        return pltpu.make_async_copy(three.at[i, h], outs[i].at[:, cols(h)], sems3.at[i, h])

    def send4(i, h):
        return pltpu.make_async_copy(four.at[i, h], pay_hbm.at[h, 64 * i + 64 : 64 * i + 128, :], sems4.at[i, h])

    every = [(i, h) for h in range(HEADS) for i in range(2)]
    for i, h in every:
        fetch(i, h).start()
    for i, h in every:
        fetch(i, h).wait()
        three[i, h] = 0.125 * pool_eight(rows.at[i, h])
        send3(i, h).start()
        four[i, h] = pool_pairs(three.at[i, h], 64)
        send4(i, h).start()
        x7 = four[i, h, pl.ds(0, 8, stride=8), :]
        for k in range(1, 8):
            x7 = x7 + four[i, h, pl.ds(k, 8, stride=8), :]
        more[i] = 0.125 * x7
        x8 = pool_pairs(more.at[i], 4)
        x8_ref[h, 4 * i : 4 * i + 4, :] = x8
        x9_ref[h, 2 * i : 2 * i + 2, :] = jnp.concatenate(
            [0.5 * (x8[0:1] + x8[1:2]), 0.5 * (x8[2:3] + x8[3:4])], axis=0
        )
    for i, h in every:
        send3(i, h).wait()
        send4(i, h).wait()


def pool_kv_call(k, v):
    anywhere = pl.BlockSpec(memory_space=pl.ANY)
    vmem = pl.BlockSpec(memory_space=pltpu.VMEM)
    return pl.pallas_call(
        pool_kv_body,
        name="pool_keys",
        in_specs=[anywhere] * 2,
        out_specs=[anywhere] * 3 + [vmem] * 2,
        out_shape=[
            pltpu.HBM((128, HEADS * WIDTH), F32),
            pltpu.HBM((128, HEADS * WIDTH), F32),
            pltpu.HBM((HEADS, PACK, WIDTH), F32),
            jax.ShapeDtypeStruct((HEADS, 8, WIDTH), F32),
            jax.ShapeDtypeStruct((HEADS, 4, WIDTH), F32),
        ],
        scratch_shapes=[
            pltpu.VMEM((2, HEADS, ROWS, WIDTH), F32),
            pltpu.VMEM((2, HEADS, 128, WIDTH), F32),
            pltpu.VMEM((2, HEADS, 64, WIDTH), F32),
            pltpu.VMEM((2, 8, WIDTH), F32),
            pltpu.SemaphoreType.DMA((2, HEADS)),
            pltpu.SemaphoreType.DMA((2, HEADS)),
            pltpu.SemaphoreType.DMA((2, HEADS)),
        ],
        compiler_params=params(20),
        cost_estimate=pl.CostEstimate(flops=2 << 20, bytes_accessed=10 << 20, transcendentals=0),
    )(in_hbm(k), in_hbm(v))


def pool_q_body(q_hbm, pay_in, q3_hbm, pay_hbm, rows, three, four, sems, sems3, sems4):
    def cols(h):
        return slice(WIDTH * h, WIDTH * h + WIDTH)

    def fetch(h):
        return pltpu.make_async_copy(q_hbm.at[:, cols(h)], rows.at[h], sems.at[h])

    def send3(h):
        return pltpu.make_async_copy(three.at[h], q3_hbm.at[:, cols(h)], sems3.at[h])

    def send4(h):
        return pltpu.make_async_copy(four.at[h], pay_hbm.at[h, 0:64, :], sems4.at[h])

    for h in range(HEADS):
        fetch(h).start()
    for h in range(HEADS):
        fetch(h).wait()
        three[h] = (0.125 * SCALE) * pool_eight(rows.at[h])
        send3(h).start()
        four[h] = pool_pairs(three.at[h], 64)
        send4(h).start()
    for h in range(HEADS):
        send3(h).wait()
        send4(h).wait()


def pool_q_call(q, pay):
    anywhere = pl.BlockSpec(memory_space=pl.ANY)
    return pl.pallas_call(
        pool_q_body,
        name="pool_queries",
        in_specs=[anywhere] * 2,
        out_specs=[anywhere] * 2,
        out_shape=[pltpu.HBM((128, HEADS * WIDTH), F32), pltpu.HBM((HEADS, PACK, WIDTH), F32)],
        input_output_aliases={1: 1},
        scratch_shapes=[
            pltpu.VMEM((HEADS, ROWS, WIDTH), F32),
            pltpu.VMEM((HEADS, 128, WIDTH), F32),
            pltpu.VMEM((HEADS, 64, WIDTH), F32),
            pltpu.SemaphoreType.DMA((HEADS,)),
            pltpu.SemaphoreType.DMA((HEADS,)),
            pltpu.SemaphoreType.DMA((HEADS,)),
        ],
        compiler_params=params(),
        cost_estimate=pl.CostEstimate(flops=2 << 30, bytes_accessed=5 << 20, transcendentals=0),
    )(in_hbm(q), in_hbm(pay))


def pack_body(pay_hbm, r8_ref, r9a_ref, r9b_ref, out_hbm, rows, sem):
    rows[:, 0:8, :] = r8_ref[...]
    rows[:, 8:12, :] = r9a_ref[...]
    rows[:, 12:16, :] = r9b_ref[...]
    copy = pltpu.make_async_copy(rows, out_hbm.at[:, 192:208, :], sem)
    copy.start()
    copy.wait()


def pack_call(pay, r8, r9a, r9b):
    vmem = pl.BlockSpec(memory_space=pltpu.VMEM)
    anywhere = pl.BlockSpec(memory_space=pl.ANY)
    return pl.pallas_call(
        pack_body,
        name="pack_rows",
        in_specs=[anywhere, vmem, vmem, vmem],
        out_specs=anywhere,
        out_shape=pltpu.HBM((HEADS, PACK, WIDTH), F32),
        input_output_aliases={0: 0},
        scratch_shapes=[pltpu.VMEM((HEADS, 16, WIDTH), F32), pltpu.SemaphoreType.DMA],
        compiler_params=params(4),
        cost_estimate=pl.CostEstimate(flops=0, bytes_accessed=1 << 17, transcendentals=0),
    )(in_hbm(pay), r8, r9a, r9b)


def local_body(count, q_ref, k_ref, v_ref, o_ref, lse_ref, columns):
    head = pl.program_id(0)

    def load(ref):
        return [ref[pl.ds(k, 128, stride=8), :] for k in range(8)]

    def pool(parts):
        return [0.5 * (parts[2 * i] + parts[2 * i + 1]) for i in range(len(parts) // 2)]

    def rows(parts, begin, count):
        return jnp.concatenate([x[begin : begin + count] for x in parts], axis=0)

    q0 = [x * SCALE for x in load(q_ref)]
    k0, v0 = load(k_ref), load(v_ref)
    q1, k1, v1 = pool(q0), pool(k0), pool(v0)
    q2, k2, v2 = pool(q1), pool(k1), pool(v1)
    tasks = []
    for p in range(4):
        c = 32 * p
        tasks.append((rows(q0, c, 32), rows(k0, c, 32), rows(v0, c, 32), 0))
    for p in range(4):
        c = 32 * (p ^ 1)
        tasks.append((rows(q1, 32 * p, 32), rows(k1, c, 32), rows(v1, c, 32), 1))
    for b in range(2):
        c = 64 * (b ^ 1)
        tasks.append((rows(q2, 64 * b, 64), rows(k2, c, 64), rows(v2, c, 64), 2))
    done = attend_all(tasks)
    at0, at1, at2 = done[:4], done[4:8], done[8:]

    lane = lax.broadcasted_iota(jnp.int32, (128, WIDTH), 1)
    lses = [[None] * 4 for _ in range(8)]
    for p in range(4):
        off = 32 * (p % 2)
        for j in range(4):
            i = j // 2
            one = tuple(x[32 * j : 32 * j + 32] for x in at1[p])
            two = tuple(x[64 * i + off : 64 * i + off + 32] for x in at2[p // 2])
            coarse = merge(one, two)
            for k in (2 * j, 2 * j + 1):
                m, s, n = merge(tuple(x[32 * k : 32 * k + 32] for x in at0[p]), coarse)
                o_ref[128 * k + 32 * p : 128 * k + 32 * p + 32, :] = n / s
                lses[k][p] = m + jnp.log2(s)
    for k in range(8):
        old = columns[128 * k : 128 * k + 128, :]
        columns[128 * k : 128 * k + 128, :] = jnp.where(lane == head, jnp.concatenate(lses[k], axis=0), old)

    @pl.when(head == count - 1)
    def _():
        for k in range(8):
            lse_ref[:, 128 * k : 128 * k + 128] = jnp.transpose(columns[128 * k : 128 * k + 128, :])[0:8]


def local_call(q, k, v, first, count, weight):
    block = pl.BlockSpec((ROWS, WIDTH), lambda h: (0, h + first))
    return pl.pallas_call(
        functools.partial(local_body, count),
        name="local_levels",
        grid=(count,),
        in_specs=[block] * 3,
        out_specs=[pl.BlockSpec((ROWS, WIDTH), lambda h: (0, h)), pl.BlockSpec((HEADS, ROWS), lambda h: (0, 0))],
        out_shape=[
            pltpu.HBM((ROWS, count * WIDTH), F32),
            pltpu.HBM((HEADS, ROWS), F32),
        ],
        scratch_shapes=[pltpu.VMEM((ROWS, WIDTH), F32)],
        compiler_params=params(16),
        cost_estimate=pl.CostEstimate(
            flops=count * weight << 20, bytes_accessed=count * weight << 11, transcendentals=count * weight << 9
        ),
    )(in_hbm(q), in_hbm(k), in_hbm(v))


def rise_body(got_ref, six_ref, seven_ref, scratch):
    for i in range(2):
        for s in range(8):
            scratch[i, 64 * s : 64 * s + 64, :] = got_ref[s, 64 * (i + 1) : 64 * (i + 2), :]
            scratch[i, 640 + 4 * s : 644 + 4 * s, :] = got_ref[s, 192 + 4 * i : 196 + 4 * i, :]
            for j in range(2):
                begin = 200 + 4 * j + 2 * i
                place = 672 + 16 * j + 2 * s
                scratch[i, place : place + 2, :] = got_ref[s, begin : begin + 2, :]
        x6 = scratch[i, pl.ds(0, 128, stride=4), :]
        for k in range(1, 4):
            x6 = x6 + scratch[i, pl.ds(k, 128, stride=4), :]
        x6 = 0.25 * x6
        scratch[i, 512:640, :] = x6
        six_ref[i, 0:128, :] = x6
        seven_ref[i, 0:64, :] = 0.5 * (
            scratch[i, pl.ds(512, 64, stride=2), :] + scratch[i, pl.ds(513, 64, stride=2), :]
        )
        six_ref[i, 128:192, :] = scratch[i, 640:704, :]
        seven_ref[i, 64:128, :] = scratch[i, 640:704, :]


def rise_call(got):
    return pl.pallas_call(
        rise_body,
        name="rise_rows",
        out_shape=[jax.ShapeDtypeStruct((2, n, WIDTH), F32) for n in (192, 128)],
        scratch_shapes=[pltpu.VMEM((2, 704, WIDTH), F32)],
        compiler_params=params(),
        cost_estimate=pl.CostEstimate(flops=1 << 18, bytes_accessed=1 << 19, transcendentals=0),
    )(got)


def middle_body(got_ref, o_ref, lse_ref, q_ref, scratch, es):
    for i in range(3):
        for s in range(8):
            scratch[i, 64 * s : 64 * s + 64, :] = got_ref[s, 64 * i : 64 * i + 64, :]
        base, count = 0, 256
        while count >= (16 if i == 0 else 256):
            x = pool_pairs(scratch.at[i, base : base + 2 * count], count)
            base = base + 2 * count
            scratch[i, base : base + count, :] = x
            count = count // 2
    q_ref[...] = scratch[0, 768:1008, :]
    tasks = []
    for level, base, blocks in ((4, 0, 4), (5, 512, 2)):
        for g in range(blocks):
            mine = slice(base + 128 * g, base + 128 * g + 128)
            other = slice(base + 128 * (g ^ 1), base + 128 * (g ^ 1) + 128)
            tasks.append((scratch[0, mine, :], scratch[1, other, :], scratch[2, other, :], level))
    done = attend_all(tasks)
    four, five = (tuple(jnp.concatenate(x, axis=0) for x in zip(*few)) for few in (done[0:4], done[4:6]))
    for i, x in enumerate(five):
        x = jnp.broadcast_to(x, (256, WIDTH))
        for c in range(2):
            es[i, pl.ds(c, 256, stride=2), :] = x
    m, s, n = merge(four, (es[0], es[1], es[2]))
    o_ref[...] = n / s
    lse_ref[...] = m + jnp.log2(s)


def middle_call(got):
    return pl.pallas_call(
        middle_body,
        name="middle_levels",
        out_shape=[jax.ShapeDtypeStruct((n, WIDTH), F32) for n in (512, 512, 240)],
        scratch_shapes=[pltpu.VMEM((3, 1024, WIDTH), F32), pltpu.VMEM((3, 512, WIDTH), F32)],
        compiler_params=params(),
        cost_estimate=pl.CostEstimate(flops=1 << 20, bytes_accessed=1 << 16, transcendentals=1 << 10),
    )(got)


def far_body(o_ref, lse_ref, q_ref, here_ref, six_ref, core_ref, seven_ref, out_ref, es):
    def sibling(i, level):
        if level == 6:
            return six_ref[i, 0:128, :]
        if level == 7:
            return jnp.concatenate([core_ref[i, 0:64, :], seven_ref[i, 0:64, :]], axis=0)
        low = 64 + 32 * (level - 8)
        return jnp.concatenate(
            [
                here_ref[i, 64 + low : 96 + low, :],
                core_ref[i, low : low + 32, :],
                six_ref[i, 64 + low : 96 + low, :],
                seven_ref[i, low : low + 32, :],
            ],
            axis=0,
        )

    tasks = []
    base, count = 0, 128
    for level in range(6, 10):
        tasks.append((q_ref[base : base + count, :], sibling(0, level), sibling(1, level), level))
        base, count = base + count, count // 2
    levels = attend_all(tasks)

    def spread(i, base, x, times):
        n = x.shape[0]
        x = jnp.broadcast_to(x, (n, WIDTH))
        for c in range(times):
            es[i, pl.ds(base + c, n, stride=times), :] = x
        return es[i, base : base + times * n, :]

    running = levels[-1]
    base = 0
    for finer in reversed(levels[:-1]):
        n = running[0].shape[0]
        running = merge(finer, tuple(spread(i, base, x, 2) for i, x in enumerate(running)))
        base = base + 2 * n
    m, s, n = running
    high_o, high_lse = spread(0, 256, n / s, 4), spread(1, 256, m + jnp.log2(s), 4)
    low_o, low_lse = o_ref[...], lse_ref[...]
    top = jnp.maximum(low_lse, high_lse)
    lse = top + jnp.log2(jnp.exp2(low_lse - top) + jnp.exp2(high_lse - top))
    o = high_o + (low_o - high_o) * share(low_lse, high_lse)
    for g in range(4):
        row = jnp.transpose(lse[128 * g : 128 * g + 128])[0:8]
        for d in range(2):
            out_ref[2 * g + d, 0:64, :] = o[128 * g + 64 * d : 128 * g + 64 * d + 64]
            out_ref[2 * g + d, 64:72, :] = row if d == 0 else pltpu.roll(row, 64, 1)


def far_call(middle, here, six, core, seven):
    return pl.pallas_call(
        far_body,
        name="far_levels",
        out_shape=pltpu.HBM((HEADS, BACK, WIDTH), F32),
        scratch_shapes=[pltpu.VMEM((3, 768, WIDTH), F32)],
        compiler_params=params(),
        cost_estimate=pl.CostEstimate(flops=100 << 20, bytes_accessed=1 << 20, transcendentals=1 << 17),
    )(*middle, here, six, core, seven)


def near_body(q3_ref, k3_ref, v3_ref, o_ref, lse_ref):
    lane = lax.broadcasted_iota(jnp.int32, (128, WIDTH), 1)
    packed = jnp.zeros((128, WIDTH), F32)
    cols = [slice(WIDTH * h, WIDTH * h + WIDTH) for h in range(HEADS)]
    done = attend_all([(q3_ref[:, c], k3_ref[:, c], v3_ref[:, c], 3) for c in cols])
    for h, (m, s, n) in enumerate(done):
        o_ref[:, cols[h]] = n / s
        packed = jnp.where(lane == h, m + jnp.log2(s), packed)
    lse_ref[...] = packed


def near_call(q3, k3, v3):
    return pl.pallas_call(
        near_body,
        name="near_level",
        out_shape=[pltpu.HBM((128, HEADS * WIDTH), F32), pltpu.HBM((128, WIDTH), F32)],
        compiler_params=params(),
        cost_estimate=pl.CostEstimate(flops=200 << 20, bytes_accessed=2 << 20, transcendentals=1 << 17),
    )(in_hbm(q3), k3, v3)


def join_body(*refs):
    n = len(CALLS)
    own_hbm, own_lse_hbm = refs[:n], refs[n : 2 * n]
    o3_hbm, lse3_hbm, far_ref, out_hbm = refs[2 * n : 2 * n + 4]
    own, own_lse, shares, o3, lse3, wide, stage, own_sems, sems, out_sems = refs[2 * n + 4 :]
    place = [(call, i) for call, count in enumerate(CALLS) for i in range(count)]
    late = range(CALLS[0], HEADS)

    def cols(h):
        return slice(WIDTH * h, WIDTH * h + WIDTH)

    def fetch(h):
        call, i = place[h]
        j = h - CALLS[0]
        return pltpu.make_async_copy(own_hbm[call].at[:, cols(i)], own.at[j], own_sems.at[j])

    def results(h, part):
        if h in late:
            return own[h - CALLS[0], part, :]
        return own_hbm[0][part, cols(h)]

    def send(h):
        return pltpu.make_async_copy(stage.at[h % 4], out_hbm.at[:, cols(h)], out_sems.at[h % 4])

    others = [pltpu.make_async_copy(lse3_hbm, lse3, sems.at[0]), pltpu.make_async_copy(o3_hbm, o3, sems.at[1])]
    others += [pltpu.make_async_copy(own_lse_hbm[call], own_lse.at[call], sems.at[call + 2]) for call in range(n)]
    for copy in others:
        copy.start()
    for h in late:
        fetch(h).start()

    for h in range(HEADS):
        wide[1, h : h + 1, :] = far_ref[h, 64:65, :]
    far_lse = jnp.transpose(wide[1])[0:64]
    for c in range(2):
        wide[0, pl.ds(c, 64, stride=2), :] = far_lse
    far_lse = wide[0]
    for copy in others:
        copy.wait()
    near_lse = lse3[...]
    top = jnp.maximum(far_lse, near_lse)
    rest_lse = top + jnp.log2(jnp.exp2(far_lse - top) + jnp.exp2(near_lse - top))
    near_share = share(near_lse, far_lse)
    for h in range(HEADS):
        call, i = place[h]
        own_lse[n, h : h + 1, :] = own_lse[call, i : i + 1, :]
    for k in range(8):
        part = slice(128 * k, 128 * k + 128)
        lse = jnp.concatenate([own_lse[n, :, part], jnp.zeros((120, WIDTH), F32)], axis=0)
        shares[part, :] = share(jnp.transpose(lse), rest_lse)

    for h in range(HEADS):
        for c in range(2):
            wide[2 + h % 2, pl.ds(c, 64, stride=2), :] = far_ref[h, 0:64, :]
        far = wide[2 + h % 2]
        rest = far + (o3[:, cols(h)] - far) * jnp.broadcast_to(near_share[:, h : h + 1], (128, WIDTH))
        if h in late:
            fetch(h).wait()
        if h >= 4:
            send(h - 4).wait()
        for k in range(8):
            part = slice(128 * k, 128 * k + 128)
            weight = jnp.broadcast_to(shares[part, h : h + 1], (128, WIDTH))
            stage[h % 4, pl.ds(k, 128, stride=8), :] = rest + (results(h, part) - rest) * weight
        send(h).start()
    for h in range(HEADS - 4, HEADS):
        send(h).wait()


def join_call(own, o3, lse3, far):
    n = len(CALLS)
    vmem = pl.BlockSpec(memory_space=pltpu.VMEM)
    anywhere = pl.BlockSpec(memory_space=pl.ANY)
    return pl.pallas_call(
        join_body,
        name="join_levels",
        in_specs=[vmem] + [anywhere] * (2 * n + 1) + [vmem],
        out_specs=anywhere,
        out_shape=pltpu.HBM((ROWS, HEADS * WIDTH), F32),
        scratch_shapes=[
            pltpu.VMEM((HEADS - CALLS[0], ROWS, WIDTH), F32),
            pltpu.VMEM((n + 1, HEADS, ROWS), F32),
            pltpu.VMEM((ROWS, WIDTH), F32),
            pltpu.VMEM((128, HEADS * WIDTH), F32),
            pltpu.VMEM((128, WIDTH), F32),
            pltpu.VMEM((4, 128, WIDTH), F32),
            pltpu.VMEM((4, ROWS, WIDTH), F32),
            pltpu.SemaphoreType.DMA((HEADS - CALLS[0],)),
            pltpu.SemaphoreType.DMA((n + 2,)),
            pltpu.SemaphoreType.DMA((4,)),
        ],
        compiler_params=params(14),
        cost_estimate=pl.CostEstimate(flops=16 << 20, bytes_accessed=9 << 20, transcendentals=1 << 20),
    )(own[0][0], *[in_hbm(o) for o, _ in own[1:]], *[in_hbm(lse) for _, lse in own], in_hbm(o3), in_hbm(lse3), far)


def hop(x, axis, flip):
    return lax.ppermute(x, axis, [(i, i ^ flip) for i in range(lax.axis_size(axis))])


def transpose_heads(x):
    return lax.all_to_all(x, "node", 0, 0, axis_index_groups=GROUPS, tiled=True)


def on_device(queries, keys, values):
    k3, v3, pay, x8, x9 = pool_kv_call(keys, values)
    sib_k3 = hop(k3, "node", 1)
    first = [sum(CALLS[:i]) for i in range(len(CALLS))]
    local = []

    def local_part(i, *after, weight=1024):
        q, k, v = lax.optimization_barrier((queries, keys, values) + after)[:3]
        return local_call(q, k, v, first[i], CALLS[i], weight)

    r8, r9a, r9b = hop(x8, "seq", 2), hop(x9, "seq", 4), hop(x9, "seq", 6)
    q3, pay = pool_q_call(queries, pay)
    pay = pack_call(pay, r8, r9a, r9b)
    got = transpose_heads(pay)
    part = local_part(0, pay, weight=1)
    got, part = lax.optimization_barrier((got, part))
    local.append(part)
    v3 = lax.optimization_barrier((part, v3))[1]
    sib_v3 = hop(v3, "node", 1)

    here6, here7 = rise_call(got)
    six = hop(here6, "node", 12)
    core = hop(here7, "seq", 1)
    seven = hop(core, "node", 12)
    middle = middle_call(lax.optimization_barrier((got, core))[0])
    part = local_part(1, core, weight=1)
    six, seven, part, middle = lax.optimization_barrier((six, seven, part, middle))
    local.append(part)

    far = far_call(middle, here6, six, core, seven)
    back = transpose_heads(far)
    local.append(local_part(2, far, sib_k3))
    q3 = lax.optimization_barrier((q3, local[-1]))[0]
    o3, lse3 = near_call(q3, sib_k3, sib_v3)
    return join_call(local, o3, lse3, back)


def solution(mesh):
    spec = P(("seq", "node"), None)
    return jax.shard_map(on_device, mesh=mesh, in_specs=(spec, spec, spec), out_specs=spec, check_vma=False)
```

```python
import functools
import math

import jax
import jax.numpy as jnp
from jax import lax
from jax.experimental import pallas as pl
from jax.experimental.pallas import tpu as pltpu
from jax.sharding import PartitionSpec as P

HEADS = 8
PACK = 208
BACK = 72
CALLS = (5, 2, 1)
WIDTH = 128
ROWS = 1024
F32 = jnp.float32
BF16 = jnp.bfloat16
SCALE = WIDTH ** (-0.5) / math.log(2.0)
MIB = 1024 * 1024

GROUPS = [list(range(8)), [12, 13, 14, 15, 8, 9, 10, 11]]


def params(mib=12):
    return pltpu.CompilerParams(vmem_limit_bytes=mib * MIB)


def in_hbm(x):
    return pltpu.with_memory_space_constraint(x, pltpu.HBM)


def split(x):
    hi = x.astype(BF16)
    lo = (x - hi.astype(F32)).astype(BF16)
    return hi, lo


def dot_nt(a, b):
    return lax.dot_general(a, b, (((1,), (1,)), ((), ())), preferred_element_type=F32)


def dot_nn(a, b):
    return lax.dot_general(a, b, (((1,), (0,)), ((), ())), preferred_element_type=F32)


def key_side(k):
    hi, lo = split(k)
    return jnp.concatenate([hi, hi], axis=1), jnp.concatenate([lo, jnp.zeros_like(lo)], axis=1)


def scores(q, sides):
    hi, lo = split(q)
    both = jnp.concatenate([hi, lo], axis=1)
    first, second = sides
    n = first.shape[0]
    if n == 128:
        s = dot_nt(both, jnp.concatenate([first, second], axis=0))
        return s[:, :n] + s[:, n:]
    return dot_nt(both, first) + dot_nt(both, second)


def weigh(p, side):
    hi, lo = side
    p_hi, p_lo = p
    if hi.shape[0] == 128:
        left = jnp.concatenate([p_hi, p_lo], axis=1)
        right = jnp.concatenate(
            [jnp.concatenate([hi, lo], axis=1), jnp.concatenate([hi, jnp.zeros_like(lo)], axis=1)], axis=0
        )
        r = dot_nn(left, right)
        return r[:, :WIDTH] + r[:, WIDTH:]
    r = dot_nn(p_hi, jnp.concatenate([hi, lo], axis=1))
    return r[:, :WIDTH] + r[:, WIDTH:] + dot_nn(p_lo, hi)


def attend_all(tasks):
    grids = [scores(q, key_side(k)) for q, k, _, _ in tasks]
    peaks = [jnp.max(s, axis=1, keepdims=True) for s in grids]
    weights = [jnp.exp2(s - peak) for s, peak in zip(grids, peaks)]
    totals = [jnp.sum(p, axis=1, keepdims=True) for p in weights]
    halves = [split(p) for p in weights]
    numerators = [weigh(p, split(task[2])) for p, task in zip(halves, tasks)]
    return [(peak + float(task[3]), t, n) for peak, t, n, task in zip(peaks, totals, numerators, tasks)]


def merge(a, b):
    ma, sa, na = a
    mb, sb, nb = b
    m = jnp.maximum(ma, mb)
    fa, fb = jnp.exp2(ma - m), jnp.exp2(mb - m)
    return m, sa * fa + sb * fb, na * fa + nb * fb


def share(a, b):
    return 1.0 / (1.0 + jnp.exp2(b - a))


def pool_eight(ref):
    total = ref[pl.ds(0, 128, stride=8), :]
    for k in range(1, 8):
        total = total + ref[pl.ds(k, 128, stride=8), :]
    return total


def pool_pairs(ref, n):
    return 0.5 * (ref[pl.ds(0, n, stride=2), :] + ref[pl.ds(1, n, stride=2), :])


def pool_kv_body(k_hbm, v_hbm, k3_hbm, v3_hbm, pay_hbm, x8_ref, x9_ref, rows, three, four, more, sems, sems3, sems4):
    arrays, outs = (k_hbm, v_hbm), (k3_hbm, v3_hbm)

    def cols(h):
        return slice(WIDTH * h, WIDTH * h + WIDTH)

    def fetch(i, h):
        return pltpu.make_async_copy(arrays[i].at[:, cols(h)], rows.at[i, h], sems.at[i, h])

    def send3(i, h):
        return pltpu.make_async_copy(three.at[i, h], outs[i].at[:, cols(h)], sems3.at[i, h])

    def send4(i, h):
        return pltpu.make_async_copy(four.at[i, h], pay_hbm.at[h, 64 * i + 64 : 64 * i + 128, :], sems4.at[i, h])

    every = [(i, h) for h in range(HEADS) for i in range(2)]
    for i, h in every:
        fetch(i, h).start()
    for i, h in every:
        fetch(i, h).wait()
        three[i, h] = 0.125 * pool_eight(rows.at[i, h])
        send3(i, h).start()
        four[i, h] = pool_pairs(three.at[i, h], 64)
        send4(i, h).start()
        x7 = four[i, h, pl.ds(0, 8, stride=8), :]
        for k in range(1, 8):
            x7 = x7 + four[i, h, pl.ds(k, 8, stride=8), :]
        more[i] = 0.125 * x7
        x8 = pool_pairs(more.at[i], 4)
        x8_ref[h, 4 * i : 4 * i + 4, :] = x8
        x9_ref[h, 2 * i : 2 * i + 2, :] = jnp.concatenate(
            [0.5 * (x8[0:1] + x8[1:2]), 0.5 * (x8[2:3] + x8[3:4])], axis=0
        )
    for i, h in every:
        send3(i, h).wait()
        send4(i, h).wait()


def pool_kv_call(k, v):
    anywhere = pl.BlockSpec(memory_space=pl.ANY)
    vmem = pl.BlockSpec(memory_space=pltpu.VMEM)
    return pl.pallas_call(
        pool_kv_body,
        name="pool_keys",
        in_specs=[anywhere] * 2,
        out_specs=[anywhere] * 3 + [vmem] * 2,
        out_shape=[
            pltpu.HBM((128, HEADS * WIDTH), F32),
            pltpu.HBM((128, HEADS * WIDTH), F32),
            pltpu.HBM((HEADS, PACK, WIDTH), F32),
            jax.ShapeDtypeStruct((HEADS, 8, WIDTH), F32),
            jax.ShapeDtypeStruct((HEADS, 4, WIDTH), F32),
        ],
        scratch_shapes=[
            pltpu.VMEM((2, HEADS, ROWS, WIDTH), F32),
            pltpu.VMEM((2, HEADS, 128, WIDTH), F32),
            pltpu.VMEM((2, HEADS, 64, WIDTH), F32),
            pltpu.VMEM((2, 8, WIDTH), F32),
            pltpu.SemaphoreType.DMA((2, HEADS)),
            pltpu.SemaphoreType.DMA((2, HEADS)),
            pltpu.SemaphoreType.DMA((2, HEADS)),
        ],
        compiler_params=params(20),
        cost_estimate=pl.CostEstimate(flops=2 << 20, bytes_accessed=10 << 20, transcendentals=0),
    )(in_hbm(k), in_hbm(v))


def pool_q_body(q_hbm, pay_in, q3_hbm, pay_hbm, rows, three, four, sems, sems3, sems4):
    def cols(h):
        return slice(WIDTH * h, WIDTH * h + WIDTH)

    def fetch(h):
        return pltpu.make_async_copy(q_hbm.at[:, cols(h)], rows.at[h], sems.at[h])

    def send3(h):
        return pltpu.make_async_copy(three.at[h], q3_hbm.at[:, cols(h)], sems3.at[h])

    def send4(h):
        return pltpu.make_async_copy(four.at[h], pay_hbm.at[h, 0:64, :], sems4.at[h])

    for h in range(HEADS):
        fetch(h).start()
    for h in range(HEADS):
        fetch(h).wait()
        three[h] = (0.125 * SCALE) * pool_eight(rows.at[h])
        send3(h).start()
        four[h] = pool_pairs(three.at[h], 64)
        send4(h).start()
    for h in range(HEADS):
        send3(h).wait()
        send4(h).wait()


def pool_q_call(q, pay):
    anywhere = pl.BlockSpec(memory_space=pl.ANY)
    return pl.pallas_call(
        pool_q_body,
        name="pool_queries",
        in_specs=[anywhere] * 2,
        out_specs=[anywhere] * 2,
        out_shape=[pltpu.HBM((128, HEADS * WIDTH), F32), pltpu.HBM((HEADS, PACK, WIDTH), F32)],
        input_output_aliases={1: 1},
        scratch_shapes=[
            pltpu.VMEM((HEADS, ROWS, WIDTH), F32),
            pltpu.VMEM((HEADS, 128, WIDTH), F32),
            pltpu.VMEM((HEADS, 64, WIDTH), F32),
            pltpu.SemaphoreType.DMA((HEADS,)),
            pltpu.SemaphoreType.DMA((HEADS,)),
            pltpu.SemaphoreType.DMA((HEADS,)),
        ],
        compiler_params=params(),
        cost_estimate=pl.CostEstimate(flops=2 << 30, bytes_accessed=5 << 20, transcendentals=0),
    )(in_hbm(q), in_hbm(pay))


def pack_body(pay_hbm, r8_ref, r9a_ref, r9b_ref, out_hbm, rows, sem):
    rows[:, 0:8, :] = r8_ref[...]
    rows[:, 8:12, :] = r9a_ref[...]
    rows[:, 12:16, :] = r9b_ref[...]
    copy = pltpu.make_async_copy(rows, out_hbm.at[:, 192:208, :], sem)
    copy.start()
    copy.wait()


def pack_call(pay, r8, r9a, r9b):
    vmem = pl.BlockSpec(memory_space=pltpu.VMEM)
    anywhere = pl.BlockSpec(memory_space=pl.ANY)
    return pl.pallas_call(
        pack_body,
        name="pack_rows",
        in_specs=[anywhere, vmem, vmem, vmem],
        out_specs=anywhere,
        out_shape=pltpu.HBM((HEADS, PACK, WIDTH), F32),
        input_output_aliases={0: 0},
        scratch_shapes=[pltpu.VMEM((HEADS, 16, WIDTH), F32), pltpu.SemaphoreType.DMA],
        compiler_params=params(4),
        cost_estimate=pl.CostEstimate(flops=0, bytes_accessed=1 << 17, transcendentals=0),
    )(in_hbm(pay), r8, r9a, r9b)


def local_body(count, q_ref, k_ref, v_ref, o_ref, lse_ref, columns):
    head = pl.program_id(0)

    def load(ref):
        return [ref[pl.ds(k, 128, stride=8), :] for k in range(8)]

    def pool(parts):
        return [0.5 * (parts[2 * i] + parts[2 * i + 1]) for i in range(len(parts) // 2)]

    def rows(parts, begin, count):
        return jnp.concatenate([x[begin : begin + count] for x in parts], axis=0)

    q0 = [x * SCALE for x in load(q_ref)]
    k0, v0 = load(k_ref), load(v_ref)
    q1, k1, v1 = pool(q0), pool(k0), pool(v0)
    q2, k2, v2 = pool(q1), pool(k1), pool(v1)
    tasks = []
    for p in range(4):
        c = 32 * p
        tasks.append((rows(q0, c, 32), rows(k0, c, 32), rows(v0, c, 32), 0))
    for p in range(4):
        c = 32 * (p ^ 1)
        tasks.append((rows(q1, 32 * p, 32), rows(k1, c, 32), rows(v1, c, 32), 1))
    for b in range(2):
        c = 64 * (b ^ 1)
        tasks.append((rows(q2, 64 * b, 64), rows(k2, c, 64), rows(v2, c, 64), 2))
    done = attend_all(tasks)
    at0, at1, at2 = done[:4], done[4:8], done[8:]

    lane = lax.broadcasted_iota(jnp.int32, (128, WIDTH), 1)
    lses = [[None] * 4 for _ in range(8)]
    for p in range(4):
        off = 32 * (p % 2)
        for j in range(4):
            i = j // 2
            one = tuple(x[32 * j : 32 * j + 32] for x in at1[p])
            two = tuple(x[64 * i + off : 64 * i + off + 32] for x in at2[p // 2])
            coarse = merge(one, two)
            for k in (2 * j, 2 * j + 1):
                m, s, n = merge(tuple(x[32 * k : 32 * k + 32] for x in at0[p]), coarse)
                o_ref[128 * k + 32 * p : 128 * k + 32 * p + 32, :] = n / s
                lses[k][p] = m + jnp.log2(s)
    for k in range(8):
        old = columns[128 * k : 128 * k + 128, :]
        columns[128 * k : 128 * k + 128, :] = jnp.where(lane == head, jnp.concatenate(lses[k], axis=0), old)

    @pl.when(head == count - 1)
    def _():
        for k in range(8):
            lse_ref[:, 128 * k : 128 * k + 128] = jnp.transpose(columns[128 * k : 128 * k + 128, :])[0:8]


def local_call(q, k, v, first, count, weight):
    block = pl.BlockSpec((ROWS, WIDTH), lambda h: (0, h + first))
    return pl.pallas_call(
        functools.partial(local_body, count),
        name="local_levels",
        grid=(count,),
        in_specs=[block] * 3,
        out_specs=[pl.BlockSpec((ROWS, WIDTH), lambda h: (0, h)), pl.BlockSpec((HEADS, ROWS), lambda h: (0, 0))],
        out_shape=[
            pltpu.HBM((ROWS, count * WIDTH), F32),
            pltpu.HBM((HEADS, ROWS), F32),
        ],
        scratch_shapes=[pltpu.VMEM((ROWS, WIDTH), F32)],
        compiler_params=params(16),
        cost_estimate=pl.CostEstimate(
            flops=count * weight << 20, bytes_accessed=count * weight << 11, transcendentals=count * weight << 9
        ),
    )(in_hbm(q), in_hbm(k), in_hbm(v))


def rise_body(got_ref, six_ref, seven_ref, scratch):
    for i in range(2):
        for s in range(8):
            scratch[i, 64 * s : 64 * s + 64, :] = got_ref[s, 64 * (i + 1) : 64 * (i + 2), :]
            scratch[i, 640 + 4 * s : 644 + 4 * s, :] = got_ref[s, 192 + 4 * i : 196 + 4 * i, :]
            for j in range(2):
                begin = 200 + 4 * j + 2 * i
                place = 672 + 16 * j + 2 * s
                scratch[i, place : place + 2, :] = got_ref[s, begin : begin + 2, :]
        x6 = scratch[i, pl.ds(0, 128, stride=4), :]
        for k in range(1, 4):
            x6 = x6 + scratch[i, pl.ds(k, 128, stride=4), :]
        x6 = 0.25 * x6
        scratch[i, 512:640, :] = x6
        six_ref[i, 0:128, :] = x6
        seven_ref[i, 0:64, :] = 0.5 * (
            scratch[i, pl.ds(512, 64, stride=2), :] + scratch[i, pl.ds(513, 64, stride=2), :]
        )
        six_ref[i, 128:192, :] = scratch[i, 640:704, :]
        seven_ref[i, 64:128, :] = scratch[i, 640:704, :]


def rise_call(got):
    return pl.pallas_call(
        rise_body,
        name="rise_rows",
        out_shape=[jax.ShapeDtypeStruct((2, n, WIDTH), F32) for n in (192, 128)],
        scratch_shapes=[pltpu.VMEM((2, 704, WIDTH), F32)],
        compiler_params=params(),
        cost_estimate=pl.CostEstimate(flops=1 << 18, bytes_accessed=1 << 19, transcendentals=0),
    )(got)


def middle_body(got_ref, o_ref, lse_ref, q_ref, scratch, es):
    for i in range(3):
        for s in range(8):
            scratch[i, 64 * s : 64 * s + 64, :] = got_ref[s, 64 * i : 64 * i + 64, :]
        base, count = 0, 256
        while count >= (16 if i == 0 else 256):
            x = pool_pairs(scratch.at[i, base : base + 2 * count], count)
            base = base + 2 * count
            scratch[i, base : base + count, :] = x
            count = count // 2
    q_ref[...] = scratch[0, 768:1008, :]
    tasks = []
    for level, base, blocks in ((4, 0, 4), (5, 512, 2)):
        for g in range(blocks):
            mine = slice(base + 128 * g, base + 128 * g + 128)
            other = slice(base + 128 * (g ^ 1), base + 128 * (g ^ 1) + 128)
            tasks.append((scratch[0, mine, :], scratch[1, other, :], scratch[2, other, :], level))
    done = attend_all(tasks)
    four, five = (tuple(jnp.concatenate(x, axis=0) for x in zip(*few)) for few in (done[0:4], done[4:6]))
    for i, x in enumerate(five):
        x = jnp.broadcast_to(x, (256, WIDTH))
        for c in range(2):
            es[i, pl.ds(c, 256, stride=2), :] = x
    m, s, n = merge(four, (es[0], es[1], es[2]))
    o_ref[...] = n / s
    lse_ref[...] = m + jnp.log2(s)


def middle_call(got):
    return pl.pallas_call(
        middle_body,
        name="middle_levels",
        out_shape=[jax.ShapeDtypeStruct((n, WIDTH), F32) for n in (512, 512, 240)],
        scratch_shapes=[pltpu.VMEM((3, 1024, WIDTH), F32), pltpu.VMEM((3, 512, WIDTH), F32)],
        compiler_params=params(),
        cost_estimate=pl.CostEstimate(flops=1 << 20, bytes_accessed=1 << 16, transcendentals=1 << 10),
    )(got)


def far_body(o_ref, lse_ref, q_ref, here_ref, six_ref, core_ref, seven_ref, out_ref, es):
    def sibling(i, level):
        if level == 6:
            return six_ref[i, 0:128, :]
        if level == 7:
            return jnp.concatenate([core_ref[i, 0:64, :], seven_ref[i, 0:64, :]], axis=0)
        low = 64 + 32 * (level - 8)
        return jnp.concatenate(
            [
                here_ref[i, 64 + low : 96 + low, :],
                core_ref[i, low : low + 32, :],
                six_ref[i, 64 + low : 96 + low, :],
                seven_ref[i, low : low + 32, :],
            ],
            axis=0,
        )

    tasks = []
    base, count = 0, 128
    for level in range(6, 10):
        tasks.append((q_ref[base : base + count, :], sibling(0, level), sibling(1, level), level))
        base, count = base + count, count // 2
    levels = attend_all(tasks)

    def spread(i, base, x, times):
        n = x.shape[0]
        x = jnp.broadcast_to(x, (n, WIDTH))
        for c in range(times):
            es[i, pl.ds(base + c, n, stride=times), :] = x
        return es[i, base : base + times * n, :]

    running = levels[-1]
    base = 0
    for finer in reversed(levels[:-1]):
        n = running[0].shape[0]
        running = merge(finer, tuple(spread(i, base, x, 2) for i, x in enumerate(running)))
        base = base + 2 * n
    m, s, n = running
    high_o, high_lse = spread(0, 256, n / s, 4), spread(1, 256, m + jnp.log2(s), 4)
    low_o, low_lse = o_ref[...], lse_ref[...]
    top = jnp.maximum(low_lse, high_lse)
    lse = top + jnp.log2(jnp.exp2(low_lse - top) + jnp.exp2(high_lse - top))
    o = high_o + (low_o - high_o) * share(low_lse, high_lse)
    for g in range(4):
        row = jnp.transpose(lse[128 * g : 128 * g + 128])[0:8]
        for d in range(2):
            out_ref[2 * g + d, 0:64, :] = o[128 * g + 64 * d : 128 * g + 64 * d + 64]
            out_ref[2 * g + d, 64:72, :] = row if d == 0 else pltpu.roll(row, 64, 1)


def far_call(middle, here, six, core, seven):
    return pl.pallas_call(
        far_body,
        name="far_levels",
        out_shape=pltpu.HBM((HEADS, BACK, WIDTH), F32),
        scratch_shapes=[pltpu.VMEM((3, 768, WIDTH), F32)],
        compiler_params=params(),
        cost_estimate=pl.CostEstimate(flops=100 << 20, bytes_accessed=1 << 20, transcendentals=1 << 17),
    )(*middle, here, six, core, seven)


def near_body(q3_ref, k3_ref, v3_ref, o_ref, lse_ref):
    lane = lax.broadcasted_iota(jnp.int32, (128, WIDTH), 1)
    packed = jnp.zeros((128, WIDTH), F32)
    cols = [slice(WIDTH * h, WIDTH * h + WIDTH) for h in range(HEADS)]
    done = attend_all([(q3_ref[:, c], k3_ref[:, c], v3_ref[:, c], 3) for c in cols])
    for h, (m, s, n) in enumerate(done):
        o_ref[:, cols[h]] = n / s
        packed = jnp.where(lane == h, m + jnp.log2(s), packed)
    lse_ref[...] = packed


def near_call(q3, k3, v3):
    return pl.pallas_call(
        near_body,
        name="near_level",
        out_shape=[pltpu.HBM((128, HEADS * WIDTH), F32), pltpu.HBM((128, WIDTH), F32)],
        compiler_params=params(),
        cost_estimate=pl.CostEstimate(flops=200 << 20, bytes_accessed=2 << 20, transcendentals=1 << 17),
    )(in_hbm(q3), k3, v3)


def join_body(*refs):
    n = len(CALLS)
    own_hbm, own_lse_hbm = refs[:n], refs[n : 2 * n]
    o3_hbm, lse3_hbm, far_ref, out_hbm = refs[2 * n : 2 * n + 4]
    own, own_lse, shares, o3, lse3, wide, stage, own_sems, sems, out_sems = refs[2 * n + 4 :]
    place = [(call, i) for call, count in enumerate(CALLS) for i in range(count)]
    late = range(CALLS[0], HEADS)

    def cols(h):
        return slice(WIDTH * h, WIDTH * h + WIDTH)

    def fetch(h):
        call, i = place[h]
        j = h - CALLS[0]
        return pltpu.make_async_copy(own_hbm[call].at[:, cols(i)], own.at[j], own_sems.at[j])

    def results(h, part):
        if h in late:
            return own[h - CALLS[0], part, :]
        return own_hbm[0][part, cols(h)]

    def send(h):
        return pltpu.make_async_copy(stage.at[h % 4], out_hbm.at[:, cols(h)], out_sems.at[h % 4])

    others = [pltpu.make_async_copy(lse3_hbm, lse3, sems.at[0]), pltpu.make_async_copy(o3_hbm, o3, sems.at[1])]
    others += [pltpu.make_async_copy(own_lse_hbm[call], own_lse.at[call], sems.at[call + 2]) for call in range(n)]
    for copy in others:
        copy.start()
    for h in late:
        fetch(h).start()

    for h in range(HEADS):
        wide[1, h : h + 1, :] = far_ref[h, 64:65, :]
    far_lse = jnp.transpose(wide[1])[0:64]
    for c in range(2):
        wide[0, pl.ds(c, 64, stride=2), :] = far_lse
    far_lse = wide[0]
    for copy in others:
        copy.wait()
    near_lse = lse3[...]
    top = jnp.maximum(far_lse, near_lse)
    rest_lse = top + jnp.log2(jnp.exp2(far_lse - top) + jnp.exp2(near_lse - top))
    near_share = share(near_lse, far_lse)
    for h in range(HEADS):
        call, i = place[h]
        own_lse[n, h : h + 1, :] = own_lse[call, i : i + 1, :]
    for k in range(8):
        part = slice(128 * k, 128 * k + 128)
        lse = jnp.concatenate([own_lse[n, :, part], jnp.zeros((120, WIDTH), F32)], axis=0)
        shares[part, :] = share(jnp.transpose(lse), rest_lse)

    for h in range(HEADS):
        for c in range(2):
            wide[2 + h % 2, pl.ds(c, 64, stride=2), :] = far_ref[h, 0:64, :]
        far = wide[2 + h % 2]
        rest = far + (o3[:, cols(h)] - far) * jnp.broadcast_to(near_share[:, h : h + 1], (128, WIDTH))
        if h in late:
            fetch(h).wait()
        if h >= 4:
            send(h - 4).wait()
        for k in range(8):
            part = slice(128 * k, 128 * k + 128)
            weight = jnp.broadcast_to(shares[part, h : h + 1], (128, WIDTH))
            stage[h % 4, pl.ds(k, 128, stride=8), :] = rest + (results(h, part) - rest) * weight
        send(h).start()
    for h in range(HEADS - 4, HEADS):
        send(h).wait()


def join_call(own, o3, lse3, far):
    n = len(CALLS)
    vmem = pl.BlockSpec(memory_space=pltpu.VMEM)
    anywhere = pl.BlockSpec(memory_space=pl.ANY)
    return pl.pallas_call(
        join_body,
        name="join_levels",
        in_specs=[vmem] + [anywhere] * (2 * n + 1) + [vmem],
        out_specs=anywhere,
        out_shape=pltpu.HBM((ROWS, HEADS * WIDTH), F32),
        scratch_shapes=[
            pltpu.VMEM((HEADS - CALLS[0], ROWS, WIDTH), F32),
            pltpu.VMEM((n + 1, HEADS, ROWS), F32),
            pltpu.VMEM((ROWS, WIDTH), F32),
            pltpu.VMEM((128, HEADS * WIDTH), F32),
            pltpu.VMEM((128, WIDTH), F32),
            pltpu.VMEM((4, 128, WIDTH), F32),
            pltpu.VMEM((4, ROWS, WIDTH), F32),
            pltpu.SemaphoreType.DMA((HEADS - CALLS[0],)),
            pltpu.SemaphoreType.DMA((n + 2,)),
            pltpu.SemaphoreType.DMA((4,)),
        ],
        compiler_params=params(14),
        cost_estimate=pl.CostEstimate(flops=16 << 20, bytes_accessed=9 << 20, transcendentals=1 << 20),
    )(own[0][0], *[in_hbm(o) for o, _ in own[1:]], *[in_hbm(lse) for _, lse in own], in_hbm(o3), in_hbm(lse3), far)


def hop(x, axis, flip):
    return lax.ppermute(x, axis, [(i, i ^ flip) for i in range(lax.axis_size(axis))])


def transpose_heads(x):
    return lax.all_to_all(x, "node", 0, 0, axis_index_groups=GROUPS, tiled=True)


def on_device(queries, keys, values):
    k3, v3, pay, x8, x9 = pool_kv_call(keys, values)
    sib_k3 = hop(k3, "node", 1)
    first = [sum(CALLS[:i]) for i in range(len(CALLS))]
    local = []

    def local_part(i, *after, weight=1024):
        q, k, v = lax.optimization_barrier((queries, keys, values) + after)[:3]
        return local_call(q, k, v, first[i], CALLS[i], weight)

    r8, r9a, r9b = hop(x8, "seq", 2), hop(x9, "seq", 4), hop(x9, "seq", 6)
    q3, pay = pool_q_call(queries, pay)
    pay = pack_call(pay, r8, r9a, r9b)
    got = transpose_heads(pay)
    part = local_part(0, pay, weight=1)
    got, part = lax.optimization_barrier((got, part))
    local.append(part)
    v3 = lax.optimization_barrier((part, v3))[1]
    sib_v3 = hop(v3, "node", 1)

    here6, here7 = rise_call(got)
    six = hop(here6, "node", 12)
    core = hop(here7, "seq", 1)
    seven = hop(core, "node", 12)
    middle = middle_call(lax.optimization_barrier((got, core))[0])
    part = local_part(1, core, weight=1)
    six, seven, part, middle = lax.optimization_barrier((six, seven, part, middle))
    local.append(part)

    far = far_call(middle, here6, six, core, seven)
    back = transpose_heads(far)
    local.append(local_part(2, far, sib_k3))
    q3 = lax.optimization_barrier((q3, local[-1]))[0]
    o3, lse3 = near_call(q3, sib_k3, sib_v3)
    return join_call(local, o3, lse3, back)


def solution(mesh):
    spec = P(("seq", "node"), None)
    return jax.shard_map(on_device, mesh=mesh, in_specs=(spec, spec, spec), out_specs=spec, check_vma=False)
```
